512 devices in a mesh: dp: 32 (over z, x), seq: 16 (over y, core).
Axes of the slice: x: 4, y: 8, z: 8, core: 2. Of those that a mesh axis runs over, the one named last changes fastest.
Arguments:
- hidden: bfloat16 [65536, 4096], P(('dp', 'seq')), may hold values from -6 to 6
- frozen_query: bfloat16 [65536, 2048], P(('dp', 'seq')), may hold values from -6 to 6
- frozen_key: bfloat16 [65536, 512], P(('dp', 'seq')), may hold values from -6 to 6
- frozen_value: bfloat16 [65536, 512], P(('dp', 'seq')), may hold values from -6 to 6
- upstream: bfloat16 [65536, 2048], P(('dp', 'seq')), may hold values from -0.078125 to 0.078125
- destination_group: int32 [65536], P(('dp', 'seq')), may hold values from 0 to 31, as said below
- destination_slot: int32 [65536], P(('dp', 'seq')), may hold values from 0 to 127, as said below
- segment_labels: int32 [32, 2048], P('dp', 'seq'), may hold values from 0 to 3, never falling along the last dimension, each value on 1 to 1024 neighbouring positions
- adapter_down_weight: bfloat16 [16, 4096], replicated, may hold values from -0.09375 to 0.09375
- adapter_up_weight: bfloat16 [16, 512], replicated, may hold values from -0.75 to 0.75
Outputs:
- attended: bfloat16 [65536, 2048], P(('dp', 'seq'))
- grad_down: float32 [16, 4096], replicated
- up_gradient: float32 [16, 512], replicated
The draws below stay inside these ranges and needn't reach their ends.
Inputs may be any that keep to these rules, and one draw needn't show every extreme that they name: `destination_group`: the rows of the loader device at index d along dp and s along seq go to devices of their groups with the same index s along seq. No loader device sends more than 8 rows to one group, and each sends exactly 8 to some group. `destination_slot`: each device of a group receives rows at every position 0 to 127 exactly once.
All inputs are finite; a program needn't handle non-finite values.
Results may differ from the reference program's by a relative error of at most 0.007.
Values may be sent and summed in bfloat16 or wider, within the bound.
A program may use at most 64 MiB of HBM per device.

```python
import math
import jax
import jax.numpy as jnp
import numpy as np
from jax import lax

MODEL_WIDTH = 4096
Q_HEADS = 16
KEY_VALUE_HEADS = 4
HEAD_SIZE = 128
ADAPTER_RANK = 16
TOK_DEV = 128
GROUP_TOK = 2048
ROWS = 65536
N_DP = 32
N_SEQ = 16


def route_plan(key):
    key_offsets, key_nudge, key_rows, key_slots, key_relabel = jax.random.split(key, 5)
    block_count = N_DP
    capacity = 2 * TOK_DEV // N_DP
    remainder = TOK_DEV - capacity
    share_each = remainder // (block_count - 1)
    extra_count = remainder % (block_count - 1)
    base_weights = np.array([capacity] + [share_each + (1 if i < extra_count else 0) for i in range(block_count - 1)], dtype=np.int32)
    pair_count = (block_count - 1) // 2
    reach_limit = max(min(share_each - 1, capacity - share_each - 2), 0)
    nudge_sizes = jax.random.randint(key_nudge, (N_SEQ, pair_count), -reach_limit, reach_limit + 1, dtype=jnp.int32)
    delta_weights = jnp.zeros((N_SEQ, block_count), jnp.int32)
    delta_weights = delta_weights.at[:, 1:1 + 2 * pair_count:2].set(nudge_sizes)
    delta_weights = delta_weights.at[:, 2:2 + 2 * pair_count:2].set(-nudge_sizes)
    weights = jnp.asarray(base_weights)[None, :] + delta_weights
    block_ends = jnp.cumsum(weights, axis=1)
    block_of = jnp.sum((block_ends[:, :, None] <= jnp.arange(TOK_DEV, dtype=jnp.int32)[None, None, :]).astype(jnp.int32), axis=1)
    offsets = jax.vmap(lambda subkey: jax.random.permutation(subkey, N_DP))(jax.random.split(key_offsets, N_SEQ))
    offsets = offsets.astype(jnp.int32)
    relabel = jax.vmap(lambda subkey: jax.random.permutation(subkey, N_DP))(jax.random.split(key_relabel, N_SEQ)).astype(jnp.int32)
    row_order = jax.vmap(lambda subkey: jax.random.permutation(subkey, TOK_DEV))(jax.random.split(key_rows, N_DP * N_SEQ))
    row_order = row_order.reshape(N_DP, N_SEQ, TOK_DEV).astype(jnp.int32)
    shuffle = jax.vmap(lambda subkey: jax.random.permutation(subkey, TOK_DEV))(jax.random.split(key_slots, N_DP * N_SEQ))
    shuffle = shuffle.reshape(N_DP, N_SEQ, TOK_DEV).astype(jnp.int32)
    seq_index = jnp.arange(N_SEQ, dtype=jnp.int32)[None, :, None]
    row_block = block_of[seq_index, row_order]
    row_shift = offsets[seq_index, row_block]
    source = jnp.arange(N_DP, dtype=jnp.int32)[:, None, None]
    target_group = relabel[seq_index, (source + row_shift) % N_DP]
    target_slot = shuffle[target_group, seq_index, row_order]
    return (target_group.reshape(-1).astype(jnp.int32), target_slot.reshape(-1).astype(jnp.int32))


def draw_destination_group(key, part):
    grouped, placed = route_plan(key)
    return grouped


def draw_destination_slot(key, part):
    grouped, placed = route_plan(key)
    return placed


def draw_frozen_query(key, part):
    own_key = jax.random.fold_in(key, 3)
    array_shape = (ROWS, Q_HEADS * HEAD_SIZE)
    return jnp.clip(jax.random.normal(own_key, array_shape, jnp.float32), -6.0, 6.0).astype(jnp.bfloat16)


def draw_frozen_key(key, part):
    own_key = jax.random.fold_in(key, 5)
    array_shape = (ROWS, KEY_VALUE_HEADS * HEAD_SIZE)
    return jnp.clip(jax.random.normal(own_key, array_shape, jnp.float32), -6.0, 6.0).astype(jnp.bfloat16)


def level_of(key, extent, pieces, least, high):
    factor_of = 1.0
    for dim, blocks in pieces:
        draws = jax.random.uniform(jax.random.fold_in(jax.random.fold_in(key, 6), dim), (blocks,), jnp.float32, least / len(pieces), high / len(pieces))
        factor_of = factor_of * jnp.repeat(jnp.exp(draws), extent[dim] // blocks).reshape((-1,) + (1,) * (len(extent) - 1 - dim))
    return factor_of


def profile(number_of, total, bound, lean):
    portions = [(1 << 20) // math.isqrt(standing ** lean) + 1 for standing in range(2, number_of + 1)]
    rest, given = total - bound - (number_of - 1), [1] * (number_of - 1)
    while rest > 0:
        candidates = [i for i in range(number_of - 1) if given[i] < bound]
        whole, left = sum([portions[i] for i in candidates]), rest
        for i in candidates:
            extra = min(bound - given[i], max(1, left * portions[i] // whole), rest)
            given[i] = given[i] + extra
            rest = rest - extra
    return np.array([bound] + given)


def ragged_sizes(key, count, total, reach, lean):
    if count == 2:
        one = jax.random.randint(key, (), max(1, total - reach), min(reach, total - 1) + 1)
        return jnp.stack([one, total - one])
    lengths = jnp.asarray(profile(count, total, reach, lean), jnp.int32)
    twos = (count - 1) // 2
    giver, taker = lengths[1:1 + 2 * twos:2], lengths[2:2 + 2 * twos:2]
    slack = jnp.minimum(giver - 1, reach - taker)
    moved = jax.random.randint(jax.random.fold_in(key, 1), (twos,), 0, 1 << 20) % (slack + 1)
    lengths = lengths.at[1:1 + 2 * twos:2].set(giver - moved).at[2:2 + 2 * twos:2].set(taker + moved)
    return lengths[jax.random.permutation(jax.random.fold_in(key, 2), count)]


def bell_draw(key, extent, width, bound, cuts=(), held_as=jnp.bfloat16):
    values = jax.random.normal(key, extent, jnp.float32) * width
    if len(cuts) > 0:
        values = level_of(key, extent, cuts, -0.22, 0.18) * values
    return jnp.clip(values, min=-bound, max=bound).astype(held_as)


def setup_inputs(seed: int = 0) -> dict:
    arg_keys = jax.random.split(jax.random.key(seed), 11)
    hidden = bell_draw(arg_keys[0], (ROWS, MODEL_WIDTH), 1.0, 6.0, ((0, 512),))
    frozen_query = draw_frozen_query(jax.random.fold_in(arg_keys[10], 71), 0)
    frozen_key = draw_frozen_key(jax.random.fold_in(arg_keys[10], 71), 0)
    frozen_value = bell_draw(arg_keys[3], (ROWS, KEY_VALUE_HEADS * HEAD_SIZE), 1.0, 6.0, ((0, 512),))
    upstream = bell_draw(arg_keys[4], (ROWS, Q_HEADS * HEAD_SIZE), 0.005, 0.078125, ((0, 512),))
    destination_group = draw_destination_group(jax.random.fold_in(arg_keys[10], 71), 0)
    destination_slot = draw_destination_slot(jax.random.fold_in(arg_keys[10], 71), 0)
    segment_labels = jax.vmap(lambda own: jnp.searchsorted(jnp.cumsum(ragged_sizes(own, 4, GROUP_TOK, GROUP_TOK // 2, 2)), jnp.arange(GROUP_TOK), side="right"))(jax.random.split(arg_keys[7], N_DP)).reshape((N_DP, GROUP_TOK)).astype(jnp.int32)
    adapter_down_weight = bell_draw(arg_keys[8], (ADAPTER_RANK, MODEL_WIDTH), MODEL_WIDTH ** -0.5, 0.09375)
    adapter_up_weight = bell_draw(arg_keys[9], (ADAPTER_RANK, KEY_VALUE_HEADS * HEAD_SIZE), (ADAPTER_RANK * 4) ** -0.5, 0.75)
    return dict(hidden=hidden, frozen_query=frozen_query, frozen_key=frozen_key, frozen_value=frozen_value, upstream=upstream, destination_group=destination_group, destination_slot=destination_slot, segment_labels=segment_labels, adapter_down_weight=adapter_down_weight, adapter_up_weight=adapter_up_weight)


adapter_scale = 2.0

def contract_over_rows(left, right):
    return lax.dot_general(left, right, (((0,), (0,)), ((), ())), preferred_element_type=jnp.float32)

def head_attention(queries, key_rows, value_row_block, upstream, labels):
    length, head_width = queries.shape
    scores = jnp.dot(queries, key_rows.T, preferred_element_type=jnp.float32) * (1.0 / math.sqrt(head_width))
    positions = jnp.arange(length, dtype=jnp.int32)
    allowed = (positions[None, :] <= positions[:, None]) & (labels[None, :] == labels[:, None])
    scores = jnp.where(allowed, scores, -jnp.inf)
    row_max = lax.optimization_barrier(jnp.max(scores, axis=1, keepdims=True))
    exponent = jnp.exp(scores - row_max)
    attn_weights = (exponent / lax.optimization_barrier(jnp.sum(exponent, axis=1, keepdims=True))).astype(jnp.bfloat16)
    attended = jnp.dot(attn_weights, value_row_block, preferred_element_type=jnp.float32).astype(jnp.bfloat16)
    value_grad = contract_over_rows(attn_weights, upstream).astype(jnp.bfloat16)
    return (attended, value_grad)

def group_attention(packed):
    queries, key_rows, value_row_block, upstream, labels = packed
    group_ratio = Q_HEADS // KEY_VALUE_HEADS

    def one_head(head_index):
        return head_attention(queries[:, head_index], key_rows[:, head_index // group_ratio], value_row_block[:, head_index // group_ratio], upstream[:, head_index], labels)
    attended, value_grad = lax.map(one_head, jnp.arange(Q_HEADS, dtype=jnp.int32))
    return (jnp.transpose(attended, (1, 0, 2)), jnp.transpose(value_grad, (1, 0, 2)))

def reference(hidden, frozen_query, frozen_key, frozen_value, upstream, destination_group, destination_slot, segment_labels, adapter_down_weight, adapter_up_weight):
    row_count = hidden.shape[0]
    loader_row = jnp.arange(row_count, dtype=jnp.int32)
    target = destination_group * GROUP_TOK + loader_row // TOK_DEV % N_SEQ * TOK_DEV + destination_slot
    reduced_total = lax.dot_general(hidden, adapter_down_weight, (((1,), (1,)), ((), ())), preferred_element_type=jnp.float32).astype(jnp.bfloat16)
    value_row_block = (frozen_value.astype(jnp.float32) + adapter_scale * jnp.dot(reduced_total, adapter_up_weight, preferred_element_type=jnp.float32)).astype(jnp.bfloat16)

    def arrange_rows(row_entries):
        return jnp.zeros_like(row_entries).at[target].set(row_entries)
    query_groups = arrange_rows(frozen_query).reshape(N_DP, GROUP_TOK, Q_HEADS, HEAD_SIZE)
    key_groups = arrange_rows(frozen_key).reshape(N_DP, GROUP_TOK, KEY_VALUE_HEADS, HEAD_SIZE)
    value_groups = arrange_rows(value_row_block).reshape(N_DP, GROUP_TOK, KEY_VALUE_HEADS, HEAD_SIZE)
    grad_groups = arrange_rows(upstream).reshape(N_DP, GROUP_TOK, Q_HEADS, HEAD_SIZE)
    attended_all, head_grads = lax.map(group_attention, (query_groups, key_groups, value_groups, grad_groups, segment_labels))
    attended = attended_all.reshape(row_count, Q_HEADS * HEAD_SIZE)
    value_gradients = head_grads.astype(jnp.float32).reshape(row_count, KEY_VALUE_HEADS, Q_HEADS // KEY_VALUE_HEADS, HEAD_SIZE)
    value_gradients = lax.optimization_barrier(jnp.sum(value_gradients, axis=2)).astype(jnp.bfloat16).reshape(row_count, KEY_VALUE_HEADS * HEAD_SIZE)
    reduced_gradient = (adapter_scale * lax.dot_general(value_gradients, adapter_up_weight, (((1,), (1,)), ((), ())), preferred_element_type=jnp.float32)).astype(jnp.bfloat16)
    grad_down = contract_over_rows(reduced_gradient, arrange_rows(hidden))
    up_gradient = adapter_scale * contract_over_rows(arrange_rows(reduced_total), value_gradients)
    return (attended, grad_down, up_gradient)
```

```python
import functools
import math

import jax
import jax.numpy as jnp
from jax import lax
from jax.experimental import pallas as pl
from jax.experimental.pallas import tpu as pltpu
from jax.sharding import PartitionSpec as P

MESH = pl.DeviceIdType.MESH
BF = jnp.bfloat16
F32 = jnp.float32
HEAD = 128
RANK = 16
KV = 4
RATIO = 4
ONE_LANE = 16
SLOT_LANE = 17
DOC_LANE = 18


def mm(a, b):
    return jnp.dot(a, b, preferred_element_type=F32)


def mm_t(a, b):
    return lax.dot_general(a, b, (((1,), (1,)), ((), ())), preferred_element_type=F32)


def t_mm(a, b):
    return lax.dot_general(a, b, (((0,), (0,)), ((), ())), preferred_element_type=F32)


def iota(shape, dim):
    return lax.broadcasted_iota(jnp.int32, shape, dim)


def kernel(
    ndp,
    nx,
    nseq,
    hops,
    hidden_ref,
    q_ref,
    k_ref,
    v_ref,
    up_ref,
    group_ref,
    slot_ref,
    label_ref,
    down_ref,
    upw_ref,
    att_ref,
    gdown_ref,
    upg_ref,
    sa0,
    sb0,
    sa1,
    sb1,
    ra0,
    rb0,
    ra1,
    rb1,
    wa,
    wb,
    pbuf,
    bias,
    aret,
    sret,
    rret,
    srg,
    rrg,
    rgs,
    rgr,
    ar_s,
    ar_r,
    z_r,
    x_r,
    ag_r,
    dp_send,
    dp_recv,
    ring_send,
    ring_recv,
    sib_send,
    sib_recv,
    rg_send,
    rg_recv,
    ar_send,
    ar_recv,
    pack,
    unpack,
    unpack_t,
    value_ref,
):
    tok = hidden_ref.shape[0]
    nz = ndp // nx
    ny = nseq // 2
    cap = 2 * tok // ndp
    blk = 2 * cap
    slots = ndp * blk
    back = 2 * hops
    win = (back + 1) * tok
    d = lax.axis_index("dp")
    s = lax.axis_index("seq")
    z, x = d // nx, d % nx
    y, c = s // 2, s % 2
    stride = 13 if ndp == 32 else 1

    def dp_peer(step):
        off = (step * stride) % ndp
        return ((z + off // nx) % nz) * nx + (x + off % nx) % nx

    def seq_peer(step):
        return (s + step) % nseq

    barrier = pltpu.get_barrier_semaphore()

    def greet_dp(step, carry):
        pl.semaphore_signal(barrier, inc=1, device_id=(dp_peer(step), s), device_id_type=MESH)
        return carry

    def greet_seq(step, carry):
        pl.semaphore_signal(barrier, inc=1, device_id=(d, seq_peer(step)), device_id_type=MESH)
        return carry

    lax.fori_loop(1, ndp, greet_dp, 0)
    lax.fori_loop(1, nseq, greet_seq, 0)

    def rows_of(index, size):
        return pl.ds(pl.multiple_of(index * size, size), size)

    def send_dp(src, dst, kind):
        def step(i, carry):
            p = dp_peer(i)
            pltpu.make_async_remote_copy(
                src_ref=src.at[rows_of(p, blk)],
                dst_ref=dst.at[rows_of(d, blk)],
                send_sem=dp_send.at[kind],
                recv_sem=dp_recv.at[kind],
                device_id=(p, s),
                device_id_type=MESH,
            ).start()
            return carry

        lax.fori_loop(1, ndp, step, 0)
        here = rows_of(d, blk)
        pltpu.make_async_copy(src.at[here], dst.at[here], dp_recv.at[kind]).start()

    def wait_bytes(ref, sem):
        pltpu.make_async_copy(ref, ref, sem).wait()

    def wait_sent(ref, sem):
        wait_bytes(ref.at[pl.ds(0, slots - blk)], sem)

    lane = iota((tok, tok), 1)
    sub = iota((tok, tok), 0)
    grow = jnp.broadcast_to(group_ref[...].astype(F32), (tok, tok))
    same = (grow == grow.T) & (sub < lane)
    rank = jnp.sum(jnp.where(same, 1.0, 0.0), axis=0, keepdims=True)
    place = group_ref[...].astype(F32) * cap + rank
    srow = iota((slots, tok), 0)
    half_row = (srow % blk) // cap
    slot_id = ((srow // blk) * cap + srow % cap).astype(F32)
    hit = slot_id == place
    for f in range(2):
        pack[:, f * tok : (f + 1) * tok] = jnp.where(hit & (half_row == f), 1.0, 0.0).astype(BF)

    down = jnp.concatenate(
        [down_ref[...], jnp.zeros((HEAD - RANK, down_ref.shape[1]), BF)], axis=0
    )
    reduced = mm_t(hidden_ref[...], down).astype(BF)
    upw = upw_ref[...]
    upw_full = jnp.concatenate([upw, jnp.zeros((HEAD - RANK, upw.shape[1]), BF)], axis=0)
    value = (v_ref[...].astype(F32) + 2.0 * mm(reduced, upw_full)).astype(BF)
    value_ref[...] = value
    slot_col = jnp.broadcast_to(slot_ref[...].astype(F32), (tok, tok)).T
    tile = (reduced.astype(F32) + jnp.where(lane == SLOT_LANE, slot_col + 1.0, 0.0)).astype(BF)

    def kv_cols(rows, cc):
        return rows[:, cc * HEAD : (cc + 1) * HEAD]

    keys = k_ref[...]
    xa0 = jnp.concatenate(
        [
            jnp.concatenate([kv_cols(keys, 2 * f), kv_cols(value, 2 * f), tile], axis=1)
            for f in range(2)
        ],
        axis=0,
    )
    sa0[...] = mm(pack[...], xa0).astype(BF)

    pl.semaphore_wait(barrier, ndp + nseq - 2)
    send_dp(sa0, ra0, 0)

    keys = k_ref[...]
    value = value_ref[...]
    xb0 = jnp.concatenate(
        [
            jnp.concatenate([kv_cols(keys, 2 * f + 1), kv_cols(value, 2 * f + 1)], axis=1)
            for f in range(2)
        ],
        axis=0,
    )
    sb0[...] = mm(pack[...], xb0).astype(BF)
    send_dp(sb0, rb0, 1)

    half_heads = KV * RATIO // 2
    half_width = half_heads * HEAD
    diag = iota((HEAD, half_width), 0) // RANK == iota((HEAD, half_width), 1) // HEAD
    narrow = []
    for f in range(2):
        wide = jnp.concatenate(
            [kv_cols(upw, 2 * f + h // RATIO) for h in range(half_heads)], axis=1
        ).astype(F32)
        wide = jnp.concatenate([wide] * half_heads, axis=0)
        wide = jnp.where(diag, wide, 0.0).astype(BF)
        narrow.append(mm_t(up_ref[:, f * half_width : (f + 1) * half_width], wide).astype(BF))
    quad = RATIO * HEAD

    def q_cols(cc):
        return q_ref[:, cc * quad : (cc + 1) * quad]

    xa1 = jnp.concatenate(
        [jnp.concatenate([q_cols(2 * f), narrow[f]], axis=1) for f in range(2)], axis=0
    )
    sa1[...] = mm(pack[...], xa1).astype(BF)
    send_dp(sa1, ra1, 2)
    xb1 = jnp.concatenate([q_cols(2 * f + 1) for f in range(2)], axis=0)
    sb1[...] = mm(pack[...], xb1).astype(BF)
    send_dp(sb1, rb1, 3)

    def place_of(hop, core):
        return rows_of((hops - hop) * 2 + core, tok)

    def ring(piece, buf, hop):
        return pltpu.make_async_remote_copy(
            src_ref=buf.at[place_of(hop - 1, c)],
            dst_ref=buf.at[place_of(hop, c)],
            send_sem=ring_send.at[piece, hop],
            recv_sem=ring_recv.at[piece, hop],
            device_id=(d, ((y + 1) % ny) * 2 + c),
            device_id_type=MESH,
        )

    def sibling(piece, buf, hop):
        return pltpu.make_async_remote_copy(
            src_ref=buf.at[place_of(hop, c)],
            dst_ref=buf.at[place_of(hop, c)],
            send_sem=sib_send.at[piece, hop],
            recv_sem=sib_recv.at[piece, hop],
            device_id=(d, y * 2 + 1 - c),
            device_id_type=MESH,
        )

    def sibling_arrived(piece, buf, hop):
        wait_bytes(buf.at[place_of(hop, 1 - c)], sib_recv.at[piece, hop])

    wait_bytes(ra0, dp_recv.at[0])
    got = ra0[...]
    slot_in = jnp.broadcast_to(
        got[:, 2 * HEAD + SLOT_LANE : 2 * HEAD + SLOT_LANE + 1].astype(F32), (slots, tok)
    )
    at = slot_in == (iota((slots, tok), 1) + 1).astype(F32)
    for f in range(2):
        chosen = jnp.where(at & (half_row == f), 1.0, 0.0)
        unpack[:, f * tok : (f + 1) * tok] = chosen.astype(BF)
        unpack_t[f * tok : (f + 1) * tok, :] = chosen.T.astype(BF)
    arranged = mm(unpack_t[...], got).astype(BF)
    doc_col = jnp.broadcast_to(label_ref[...].astype(F32), (tok, tok)).T
    doc = lane.astype(F32) == doc_col + float(DOC_LANE)
    own_tile = arranged[:tok, 2 * HEAD :].astype(F32)
    own_tile = jnp.where((lane == ONE_LANE) | doc, 1.0, own_tile).astype(BF)
    own = place_of(0, c)
    wa[own, :] = jnp.concatenate(
        [arranged[:tok, : 2 * HEAD], arranged[tok:, : 2 * HEAD], own_tile], axis=1
    )
    ring(0, wa, 1).start()
    sibling(0, wa, 0).start()
    wait_bytes(rb0, dp_recv.at[1])
    arranged = mm(unpack_t[...], rb0[...]).astype(BF)
    wb[own, :] = jnp.concatenate([arranged[:tok, :], arranged[tok:, :]], axis=1)
    ring(1, wb, 1).start()
    sibling(1, wb, 0).start()
    for hop in range(1, hops + 1):
        for piece, buf in enumerate((wa, wb)):
            ring(piece, buf, hop).wait_recv()
            if hop < hops:
                ring(piece, buf, hop + 1).start()
            sibling(piece, buf, hop).start()
    for hop in range(hops + 1):
        for piece, buf in enumerate((wa, wb)):
            sibling_arrived(piece, buf, hop)

    window = rows_of(c, tok)
    window = pl.ds(window.start, win)
    tiles = wa[window, 4 * HEAD :]
    doc_q = jnp.where(doc, 1.0, 0.0).astype(BF)
    together = mm_t(doc_q, tiles) > 0.5
    col = iota((tok, win), 1)
    seen = together & (col - back * tok <= iota((tok, win), 0)) & (col >= (back - s) * tok)
    bias[...] = jnp.where(seen, 0.0, -1e30)
    scale = math.log2(math.e) / math.sqrt(HEAD)

    rg_total = jnp.zeros((RANK, win), F32)
    narrow_in = []
    returned = [jnp.zeros((tok, HEAD), F32) for _ in range(2)]
    for piece, (buf, arrived) in enumerate(((wa, ra1), (wb, rb1))):
        wait_bytes(arrived, dp_recv.at[2 + piece])
        arranged = mm(unpack_t[...], arrived[...]).astype(BF)
        if piece == 0:
            narrow_in = [arranged[f * tok : (f + 1) * tok, quad:].astype(F32) for f in range(2)]
        for f in range(2):
            cc = 2 * f + piece
            key = buf[window, 2 * f * HEAD : (2 * f + 1) * HEAD]
            val = jnp.concatenate(
                [buf[window, (2 * f + 1) * HEAD : (2 * f + 2) * HEAD], tiles], axis=1
            )
            lefts = []
            for h in range(RATIO):
                head = cc * RATIO + h
                lanes = (piece * RATIO + h) * RANK
                query = arranged[f * tok : (f + 1) * tok, h * HEAD : (h + 1) * HEAD]
                scores = mm_t(query, key) * scale + bias[...]
                top = jnp.max(scores, axis=1, keepdims=True)
                weights = jnp.exp2(scores - top).astype(BF)
                pbuf[h * tok : (h + 1) * tok, :] = weights
                out = mm(weights, val)
                inv = 1.0 / out[:, HEAD + ONE_LANE : HEAD + ONE_LANE + 1]
                att_ref[:, head * HEAD : (head + 1) * HEAD] = (out[:, :HEAD] * inv).astype(BF)
                mixed = jnp.where(lane < RANK, out[:, HEAD:] * inv, 0.0)
                returned[f] = returned[f] + (pltpu.roll(mixed, lanes, 1) if lanes else mixed)
                left = narrow_in[f]
                left = pltpu.roll(left, HEAD - lanes, 1) if lanes else left
                lefts.append((left[:, :RANK] * inv).astype(BF))
            rg_total = rg_total + t_mm(jnp.concatenate(lefts, axis=0), pbuf[...])

    aret[:tok, :] = returned[0].astype(BF)
    aret[tok:, :] = returned[1].astype(BF)
    sret[...] = mm(unpack[...], aret[...]).astype(BF)
    send_dp(sret, rret, 4)

    def rg_copy(w):
        return pltpu.make_async_remote_copy(
            src_ref=rgs.at[w * RANK : (w + 1) * RANK],
            dst_ref=rgr.at[w * RANK : (w + 1) * RANK],
            send_sem=rg_send.at[w],
            recv_sem=rg_recv.at[w],
            device_id=(d, (s + nseq - back + w) % nseq),
            device_id_type=MESH,
        )

    for w in range(back):
        rgs[w * RANK : (w + 1) * RANK, :] = rg_total[:, w * tok : (w + 1) * tok].astype(BF)
    for w in range(back):
        rg_copy(w).start()
    rg_own = rg_total[:, back * tok :]
    for w in range(back):
        rg_copy(w).wait_recv()
        rg_own = rg_own + rgr[w * RANK : (w + 1) * RANK, :].astype(F32)
    rg_pad = jnp.concatenate(
        [(2.0 * rg_own).astype(BF), jnp.zeros((HEAD - RANK, tok), BF)], axis=0
    )
    srg[...] = mm_t(unpack[:, :tok], rg_pad).astype(BF)
    send_dp(srg, rrg, 5)

    share = ar_s.shape[2] // HEAD

    def put(col, rows):
        lanes = (col % share) * HEAD
        ar_s[col // share, :, lanes : lanes + HEAD] = rows

    n_down = hidden_ref.shape[1] // HEAD
    wait_bytes(rret, dp_recv.at[4])
    mixed = t_mm(pack[...], rret[...]).astype(BF)
    for f in range(2):
        full = t_mm(
            mixed[f * tok : (f + 1) * tok, :], up_ref[:, f * half_width : (f + 1) * half_width]
        )
        for g in range(2):
            total = jnp.zeros((RANK, HEAD), F32)
            for h in range(g * RATIO, (g + 1) * RATIO):
                total = total + full[h * RANK : (h + 1) * RANK, h * HEAD : (h + 1) * HEAD]
            put(n_down + 2 * f + g, 2.0 * total)
    wait_bytes(rrg, dp_recv.at[5])
    rg_rows = t_mm(pack[:, :tok], rrg[...]).astype(BF)
    grad = t_mm(rg_rows[:, :RANK], hidden_ref[...])
    for t in range(n_down):
        put(t, grad[:, t * HEAD : (t + 1) * HEAD])

    def ar_start(phase, src, dst, target):
        pltpu.make_async_remote_copy(
            src_ref=src,
            dst_ref=dst,
            send_sem=ar_send.at[phase],
            recv_sem=ar_recv.at[phase],
            device_id=target,
            device_id_type=MESH,
        ).start()

    def total_of(buf, n):
        total = buf[0]
        for i in range(1, n):
            total = total + buf[i]
        return total

    def scatter(i, carry):
        p = seq_peer(i)
        ar_start(0, ar_s.at[p], ar_r.at[s], (d, p))
        return carry

    lax.fori_loop(1, nseq, scatter, 0)
    ar_r[s] = ar_s[s]
    wait_bytes(ar_r.at[pl.ds(0, nseq - 1)], ar_recv.at[0])
    z_r[z] = total_of(ar_r, nseq)

    def over_z(i, carry):
        ar_start(1, z_r.at[z], z_r.at[z], (((z + i) % nz) * nx + x, s))
        return carry

    lax.fori_loop(1, nz, over_z, 0)
    wait_bytes(z_r.at[pl.ds(0, nz - 1)], ar_recv.at[1])
    x_r[x] = total_of(z_r, nz)

    def over_x(i, carry):
        ar_start(2, x_r.at[x], x_r.at[x], (z * nx + (x + i) % nx, s))
        return carry

    lax.fori_loop(1, nx, over_x, 0)
    wait_bytes(x_r.at[pl.ds(0, nx - 1)], ar_recv.at[2])
    ag_r[s] = total_of(x_r, nx)

    def gather(i, carry):
        ar_start(3, ag_r.at[s], ag_r.at[s], (d, seq_peer(i)))
        return carry

    lax.fori_loop(1, nseq, gather, 0)
    wait_bytes(ag_r.at[pl.ds(0, nseq - 1)], ar_recv.at[3])
    for t in range(n_down + KV):
        lanes = (t % share) * HEAD
        out, col = (gdown_ref, t) if t < n_down else (upg_ref, t - n_down)
        out[:, col * HEAD : (col + 1) * HEAD] = ag_r[t // share, :, lanes : lanes + HEAD]

    for kind, buf in enumerate((sa0, sb0, sa1, sb1, sret, srg)):
        wait_sent(buf, dp_send.at[kind])
    for piece, buf in enumerate((wa, wb)):
        for hop in range(1, hops + 1):
            ring(piece, buf, hop).wait_send()
        for hop in range(hops + 1):
            sibling(piece, buf, hop).wait_send()
    for w in range(back):
        rg_copy(w).wait_send()
    wait_bytes(ar_s.at[pl.ds(0, nseq - 1)], ar_send.at[0])
    wait_bytes(z_r.at[pl.ds(0, nz - 1)], ar_send.at[1])
    wait_bytes(x_r.at[pl.ds(0, nx - 1)], ar_send.at[2])
    wait_bytes(ag_r.at[pl.ds(0, nseq - 1)], ar_send.at[3])


def shards(nx, hops, hidden, q, k, v, up, group, slot, labels, down, upw):
    ndp = lax.axis_size("dp")
    nseq = lax.axis_size("seq")
    tok = hidden.shape[0]
    slots = 4 * tok
    back = 2 * hops
    n_tiles = (hidden.shape[1] + upw.shape[1]) // HEAD
    share = -(-n_tiles // nseq) * HEAD
    dma = pltpu.SemaphoreType.DMA
    la0, lb0, la1, lb1 = 3 * HEAD, 2 * HEAD, 5 * HEAD, 4 * HEAD
    scratch = (
        [pltpu.VMEM((slots, n), BF) for n in (la0, lb0, la1, lb1)]
        + [pltpu.VMEM((slots, n), BF) for n in (la0, lb0, la1, lb1)]
        + [
            pltpu.VMEM(((back + 2) * tok, 5 * HEAD), BF),
            pltpu.VMEM(((back + 2) * tok, 4 * HEAD), BF),
            pltpu.VMEM((RATIO * tok, (back + 1) * tok), BF),
            pltpu.VMEM((tok, (back + 1) * tok), F32),
            pltpu.VMEM((2 * tok, HEAD), BF),
        ]
        + [pltpu.VMEM((slots, HEAD), BF)] * 4
        + [pltpu.VMEM((back * RANK, tok), BF)] * 2
        + [
            pltpu.VMEM((nseq, RANK, share), F32),
            pltpu.VMEM((nseq, RANK, share), F32),
            pltpu.VMEM((ndp // nx, RANK, share), F32),
            pltpu.VMEM((nx, RANK, share), F32),
            pltpu.VMEM((nseq, RANK, share), F32),
            dma((6,)),
            dma((6,)),
            dma((2, hops + 1)),
            dma((2, hops + 1)),
            dma((2, hops + 1)),
            dma((2, hops + 1)),
            dma((back,)),
            dma((back,)),
            dma((4,)),
            dma((4,)),
            pltpu.VMEM((slots, 2 * tok), BF),
            pltpu.VMEM((slots, 2 * tok), BF),
            pltpu.VMEM((2 * tok, slots), BF),
            pltpu.VMEM((tok, KV * HEAD), BF),
        ]
    )
    vmem = pl.BlockSpec(memory_space=pltpu.VMEM)
    return pl.pallas_call(
        functools.partial(kernel, ndp, nx, nseq, hops),
        out_shape=(
            jax.ShapeDtypeStruct(q.shape, BF),
            jax.ShapeDtypeStruct(down.shape, F32),
            jax.ShapeDtypeStruct(upw.shape, F32),
        ),
        in_specs=[vmem] * 10,
        out_specs=(vmem, vmem, vmem),
        scratch_shapes=scratch,
        compiler_params=pltpu.CompilerParams(
            collective_id=0, has_side_effects=True, vmem_limit_bytes=56 * 1024 * 1024
        ),
        cost_estimate=pl.CostEstimate(
            flops=4 * 10**9, bytes_accessed=4 * 10**6, transcendentals=2400000
        ),
    )(
        hidden,
        q,
        k,
        v,
        up,
        group.reshape(1, tok),
        slot.reshape(1, tok),
        labels,
        down,
        upw,
    )


def build(mesh, nx, hops):
    rows = P(("dp", "seq"), None)
    return jax.shard_map(
        functools.partial(shards, nx, hops),
        mesh=mesh,
        in_specs=(
            rows,
            rows,
            rows,
            rows,
            rows,
            P(("dp", "seq")),
            P(("dp", "seq")),
            P("dp", "seq"),
            P(),
            P(),
        ),
        out_specs=(rows, P(), P()),
        check_vma=False,
    )


def solution(mesh):
    return build(mesh, 4, 4)
```

```python
import functools
import math

import jax
import jax.numpy as jnp
from jax import lax
from jax.experimental import pallas as pl
from jax.experimental.pallas import tpu as pltpu
from jax.sharding import PartitionSpec as P

MESH = pl.DeviceIdType.MESH
BF = jnp.bfloat16
F32 = jnp.float32
HEAD = 128
RANK = 16
KV = 4
RATIO = 4
ONE_LANE = 16
DOC_LANE = 17
SPAN = HEAD // RANK


def mm(a, b):
    return jnp.dot(a, b, preferred_element_type=F32)


def mm_t(a, b):
    return lax.dot_general(a, b, (((1,), (1,)), ((), ())), preferred_element_type=F32)


def t_mm(a, b):
    return lax.dot_general(a, b, (((0,), (0,)), ((), ())), preferred_element_type=F32)


def iota(shape, dim):
    return lax.broadcasted_iota(jnp.int32, shape, dim)


def kernel(
    ndp,
    nx,
    nseq,
    hops,
    hidden_in,
    q_in,
    k_in,
    v_in,
    up_in,
    group_ref,
    slot_ref,
    label_ref,
    down_ref,
    upw_ref,
    att_out,
    gdown_ref,
    upg_ref,
    sa0,
    sb0,
    sa1,
    sb1,
    sb2,
    ra0,
    rb0,
    ra1,
    rb1,
    rb2,
    wa,
    wb,
    pbuf,
    bias,
    aret,
    sret,
    rret,
    sx,
    rx,
    srg,
    rrg,
    rgs,
    rgr,
    g_s,
    g_r,
    g_t,
    g_a,
    u_s,
    u_r,
    u_t,
    u_a,
    dp_send,
    dp_recv,
    ring_send,
    ring_recv,
    sib_send,
    sib_recv,
    rg_send,
    rg_recv,
    ar_send,
    ar_recv,
    u_send,
    u_recv,
    small,
    unsmall,
    pack,
    unpack,
    unpack_t,
    value_ref,
    hidden_ref,
    q_ref,
    k_ref,
    v_ref,
    up_ref,
    att_ref,
    load,
):
    tok = hidden_ref.shape[0]
    loads = [
        pltpu.make_async_copy(src, dst, load.at[i])
        for i, (src, dst) in enumerate(
            (
                (hidden_in, hidden_ref),
                (k_in, k_ref),
                (v_in, v_ref),
                (q_in, q_ref),
                (up_in, up_ref),
            )
        )
    ]
    att_copy = pltpu.make_async_copy(att_ref, att_out, load.at[5])
    for copy in loads:
        copy.start()
    nz = ndp // nx
    ny = nseq // 2
    cap = 2 * tok // ndp
    blk = 2 * cap
    slots = ndp * blk
    back = 2 * hops
    win = (back + 1) * tok
    d = lax.axis_index("dp")
    s = lax.axis_index("seq")
    z, x = d // nx, d % nx
    y, c = s // 2, s % 2
    stride = 13 if ndp == 32 else 1

    def dp_peer(step):
        off = (step * stride) % ndp
        return ((z + off // nx) % nz) * nx + (x + off % nx) % nx

    def seq_peer(step):
        return (s + step) % nseq

    barrier = pltpu.get_barrier_semaphore()

    def greet_dp(step, carry):
        pl.semaphore_signal(barrier, inc=1, device_id=(dp_peer(step), s), device_id_type=MESH)
        return carry

    def greet_seq(step, carry):
        pl.semaphore_signal(barrier, inc=1, device_id=(d, seq_peer(step)), device_id_type=MESH)
        return carry

    lax.fori_loop(1, ndp, greet_dp, 0)
    lax.fori_loop(1, nseq, greet_seq, 0)

    def rows_of(index, size):
        return pl.ds(pl.multiple_of(index * size, size), size)

    def send_dp(src, dst, kind, size=blk):
        def step(i, carry):
            p = dp_peer(i)
            pltpu.make_async_remote_copy(
                src_ref=src.at[rows_of(p, size)],
                dst_ref=dst.at[rows_of(d, size)],
                send_sem=dp_send.at[kind],
                recv_sem=dp_recv.at[kind],
                device_id=(p, s),
                device_id_type=MESH,
            ).start()
            return carry

        lax.fori_loop(1, ndp, step, 0)
        here = rows_of(d, size)
        pltpu.make_async_copy(src.at[here], dst.at[here], dp_recv.at[kind]).start()

    def wait_bytes(ref, sem):
        pltpu.make_async_copy(ref, ref, sem).wait()

    def wait_sent(ref, sem, size=blk):
        wait_bytes(ref.at[pl.ds(0, (ndp - 1) * size)], sem)

    lane = iota((tok, tok), 1)
    sub = iota((tok, tok), 0)
    grow = jnp.broadcast_to(group_ref[...].astype(F32), (tok, tok))
    same = (grow == grow.T) & (sub < lane)
    rank = jnp.sum(jnp.where(same, 1.0, 0.0), axis=0, keepdims=True)
    place = group_ref[...].astype(F32) * cap + rank
    srow = iota((slots, tok), 0)
    half_row = (srow % blk) // cap
    slot_id = ((srow // blk) * cap + srow % cap).astype(F32)
    hit = slot_id == place
    for f in range(2):
        pack[:, f * tok : (f + 1) * tok] = jnp.where(hit & (half_row == f), 1.0, 0.0).astype(BF)

    n_small = slots // 2
    lines = n_small // SPAN
    per_peer = lines // ndp
    mine = iota((n_small, HEAD), 1) // RANK == iota((n_small, HEAD), 0) % SPAN

    def to_lines(rows):
        kept = jnp.where(mine, rows, 0.0).reshape(lines, SPAN, HEAD)
        return jnp.sum(kept, axis=1, keepdims=True)

    def from_lines(line):
        spread = jnp.broadcast_to(line, (lines, SPAN, HEAD)).reshape(n_small, HEAD)
        return jnp.where(mine, spread, 0.0)

    fold = (sub % RANK == lane) & (lane < RANK)
    fold = jnp.where(fold, 1.0, 0.0).astype(BF)
    small_id = iota((n_small, tok), 0).astype(F32)
    small[...] = jnp.where(small_id == place, 1.0, 0.0).astype(BF)

    down = jnp.concatenate([down_ref[...]] * SPAN, axis=0)
    loads[0].wait()
    reduced = mm_t(hidden_ref[...], down).astype(BF)
    upw = upw_ref[...]
    upw_full = jnp.concatenate([upw, jnp.zeros((HEAD - RANK, upw.shape[1]), BF)], axis=0)
    loads[2].wait()
    value = (v_ref[...].astype(F32) + 2.0 * mm(reduced, upw_full)).astype(BF)
    value_ref[...] = value
    slot_col = jnp.broadcast_to(slot_ref[...].astype(F32), (tok, tok)).T
    sx[:, 0:1, :] = to_lines(mm(small[...], reduced))
    sx[:, 1:2, :] = to_lines(mm(small[...], (slot_col + 1.0).astype(BF)))

    def kv_cols(rows, cc):
        return rows[:, cc * HEAD : (cc + 1) * HEAD]

    loads[1].wait()
    keys = k_ref[...]
    xa0 = jnp.concatenate(
        [
            jnp.concatenate([kv_cols(keys, 2 * f), kv_cols(value, 2 * f)], axis=1)
            for f in range(2)
        ],
        axis=0,
    )
    sa0[...] = mm(pack[...], xa0).astype(BF)

    pl.semaphore_wait(barrier, ndp + nseq - 2)
    send_dp(sx, rx, 6, per_peer)
    send_dp(sa0, ra0, 0)

    keys = k_ref[...]
    value = value_ref[...]
    xb0 = jnp.concatenate(
        [
            jnp.concatenate([kv_cols(keys, 2 * f + 1), kv_cols(value, 2 * f + 1)], axis=1)
            for f in range(2)
        ],
        axis=0,
    )
    sb0[...] = mm(pack[...], xb0).astype(BF)
    send_dp(sb0, rb0, 1)

    half_heads = KV * RATIO // 2
    half_width = half_heads * HEAD
    diag = iota((HEAD, half_width), 0) // RANK == iota((HEAD, half_width), 1) // HEAD
    narrow = []
    loads[4].wait()
    for f in range(2):
        wide = jnp.concatenate(
            [kv_cols(upw, 2 * f + h // RATIO) for h in range(half_heads)], axis=1
        ).astype(F32)
        wide = jnp.concatenate([wide] * half_heads, axis=0)
        wide = jnp.where(diag, wide, 0.0).astype(BF)
        narrow.append(mm_t(up_ref[:, f * half_width : (f + 1) * half_width], wide).astype(BF))
    quad = RATIO * HEAD

    def q_cols(cc):
        return q_ref[:, cc * quad : (cc + 1) * quad]

    loads[3].wait()
    xa1 = jnp.concatenate(
        [jnp.concatenate([q_cols(2 * f), narrow[f]], axis=1) for f in range(2)], axis=0
    )
    sa1[...] = mm(pack[...], xa1).astype(BF)
    send_dp(sa1, ra1, 2)
    xb1 = jnp.concatenate([q_cols(2 * f + 1) for f in range(2)], axis=0)
    sb1[...] = mm(pack[...], xb1[:, : quad // 2]).astype(BF)
    send_dp(sb1, rb1, 3)
    sb2[...] = mm(pack[...], xb1[:, quad // 2 :]).astype(BF)
    send_dp(sb2, rb2, 7)

    def place_of(hop, core):
        return rows_of((hops - hop) * 2 + core, tok)

    def ring(piece, buf, hop):
        return pltpu.make_async_remote_copy(
            src_ref=buf.at[place_of(hop - 1, c)],
            dst_ref=buf.at[place_of(hop, c)],
            send_sem=ring_send.at[piece, hop],
            recv_sem=ring_recv.at[piece, hop],
            device_id=(d, ((y + 1) % ny) * 2 + c),
            device_id_type=MESH,
        )

    def sibling(piece, buf, hop):
        return pltpu.make_async_remote_copy(
            src_ref=buf.at[place_of(hop, c)],
            dst_ref=buf.at[place_of(hop, c)],
            send_sem=sib_send.at[piece, hop],
            recv_sem=sib_recv.at[piece, hop],
            device_id=(d, y * 2 + 1 - c),
            device_id_type=MESH,
        )

    def sibling_arrived(piece, buf, hop):
        wait_bytes(buf.at[place_of(hop, 1 - c)], sib_recv.at[piece, hop])

    wait_bytes(rx, dp_recv.at[6])
    slot_in = jnp.max(from_lines(rx[:, 1:2, :]), axis=1, keepdims=True)
    slot_in = jnp.broadcast_to(slot_in, (n_small, tok))
    at_small = jnp.where(slot_in == (iota((n_small, tok), 1) + 1).astype(F32), 1.0, 0.0)
    unsmall[...] = at_small.astype(BF)
    at = jnp.broadcast_to(at_small.reshape(ndp, 1, cap, tok), (ndp, 2, cap, tok))
    at = at.reshape(slots, tok)
    for f in range(2):
        chosen = jnp.where(half_row == f, at, 0.0)
        unpack[:, f * tok : (f + 1) * tok] = chosen.astype(BF)
        unpack_t[f * tok : (f + 1) * tok, :] = chosen.T.astype(BF)
    reduced_in = t_mm(unsmall[...], from_lines(rx[:, 0:1, :]).astype(BF)).astype(BF)
    own_tile = mm(reduced_in, fold)
    wait_bytes(ra0, dp_recv.at[0])
    arranged = mm(unpack_t[...], ra0[...]).astype(BF)
    doc_col = jnp.broadcast_to(label_ref[...].astype(F32), (tok, tok)).T
    doc = lane.astype(F32) == doc_col + float(DOC_LANE)
    own_tile = jnp.where((lane == ONE_LANE) | doc, 1.0, own_tile).astype(BF)
    own = place_of(0, c)
    wa[own, :] = jnp.concatenate(
        [arranged[:tok, :], arranged[tok:, :], own_tile], axis=1
    )
    ring(0, wa, 1).start()
    sibling(0, wa, 0).start()
    wait_bytes(rb0, dp_recv.at[1])
    arranged = mm(unpack_t[...], rb0[...]).astype(BF)
    wb[own, :] = jnp.concatenate([arranged[:tok, :], arranged[tok:, :]], axis=1)
    ring(1, wb, 1).start()
    sibling(1, wb, 0).start()
    def pass_on(piece, buf, hop):
        ring(piece, buf, hop).wait_recv()
        if hop < hops:
            ring(piece, buf, hop + 1).start()
        sibling(piece, buf, hop).start()

    for hop in range(1, hops):
        pass_on(0, wa, hop)
        pass_on(1, wb, hop)
    wait_bytes(ra1, dp_recv.at[2])
    queries = mm(unpack_t[...], ra1[...]).astype(BF)
    pass_on(0, wa, hops)
    for hop in range(hops + 1):
        sibling_arrived(0, wa, hop)

    window = rows_of(c, tok)
    window = pl.ds(window.start, win)
    tiles = wa[window, 4 * HEAD :]
    doc_q = jnp.where(doc, 1.0, 0.0).astype(BF)
    together = mm_t(doc_q, tiles) > 0.5
    col = iota((tok, win), 1)
    seen = together & (col - back * tok <= iota((tok, win), 0)) & (col >= (back - s) * tok)
    bias[...] = jnp.where(seen, 0.0, -1e30)
    scale = math.log2(math.e) / math.sqrt(HEAD)

    narrow_in = [queries[f * tok : (f + 1) * tok, quad:].astype(F32) for f in range(2)]
    returned = [jnp.zeros((tok, HEAD), F32) for _ in range(2)]

    def attend(piece, buf, arranged, f, first, count):
        cc = 2 * f + piece
        key = buf[window, 2 * f * HEAD : (2 * f + 1) * HEAD]
        val = jnp.concatenate(
            [buf[window, (2 * f + 1) * HEAD : (2 * f + 2) * HEAD], tiles], axis=1
        )
        query = jnp.concatenate(
            [
                arranged[f * tok : (f + 1) * tok, h * HEAD : (h + 1) * HEAD]
                for h in range(count)
            ],
            axis=0,
        )
        scores = mm_t(query, key)
        for h in range(count):
            part = scores[h * tok : (h + 1) * tok, :] * scale + bias[...]
            top = jnp.max(part, axis=1, keepdims=True)
            pbuf[f, h * tok : (h + 1) * tok, :] = jnp.exp2(part - top).astype(BF)
        weights = pbuf[f, : count * tok, :]
        out = mm(weights, val)
        inv = 1.0 / out[:, HEAD + ONE_LANE : HEAD + ONE_LANE + 1]
        attended = (out[:, :HEAD] * inv).astype(BF)
        mixed = jnp.where(iota((count * tok, HEAD), 1) < RANK, out[:, HEAD:] * inv, 0.0)
        lefts = []
        for h in range(count):
            head = cc * RATIO + first + h
            lanes = (piece * RATIO + first + h) * RANK
            rows = slice(h * tok, (h + 1) * tok)
            att_ref[:, head * HEAD : (head + 1) * HEAD] = attended[rows]
            moved = pltpu.roll(mixed[rows], lanes, 1) if lanes else mixed[rows]
            returned[f] = returned[f] + moved
            left = narrow_in[f]
            left = pltpu.roll(left, HEAD - lanes, 1) if lanes else left
            lefts.append((left[:, :RANK] * inv[rows]).astype(BF))
        return t_mm(jnp.concatenate(lefts, axis=0), weights)

    half = RATIO // 2
    rg_total = attend(0, wa, queries, 0, 0, RATIO)
    pass_on(1, wb, hops)
    rg_total = rg_total + attend(0, wa, queries, 1, 0, RATIO)
    for hop in range(hops + 1):
        sibling_arrived(1, wb, hop)
    for arrived, kind, first in ((rb1, 3, 0), (rb2, 7, half)):
        wait_bytes(arrived, dp_recv.at[kind])
        queries = mm(unpack_t[...], arrived[...]).astype(BF)
        for f in range(2):
            rg_total = rg_total + attend(1, wb, queries, f, first, half)
    att_copy.start()

    def rg_copy(w):
        return pltpu.make_async_remote_copy(
            src_ref=rgs.at[w * RANK : (w + 1) * RANK],
            dst_ref=rgr.at[w * RANK : (w + 1) * RANK],
            send_sem=rg_send.at[w],
            recv_sem=rg_recv.at[w],
            device_id=(d, (s + nseq - back + w) % nseq),
            device_id_type=MESH,
        )

    for w in range(back):
        rgs[w * RANK : (w + 1) * RANK, :] = rg_total[:, w * tok : (w + 1) * tok].astype(BF)
    for w in range(back):
        rg_copy(w).start()
    rg_own = rg_total[:, back * tok :]

    aret[:tok, :] = returned[0].astype(BF)
    aret[tok:, :] = returned[1].astype(BF)
    sret[...] = mm(unpack[...], aret[...]).astype(BF)
    send_dp(sret, rret, 4)

    for w in range(back):
        rg_copy(w).wait_recv()
        rg_own = rg_own + rgr[w * RANK : (w + 1) * RANK, :].astype(F32)
    rg_own = jnp.concatenate([(2.0 * rg_own).astype(BF)] * SPAN, axis=0)
    srg[...] = to_lines(mm_t(unsmall[...], rg_own))
    send_dp(srg, rrg, 5, per_peer)

    def copy_start(src, dst, send, recv, target):
        pltpu.make_async_remote_copy(
            src_ref=src,
            dst_ref=dst,
            send_sem=send,
            recv_sem=recv,
            device_id=target,
            device_id_type=MESH,
        ).start()

    def to_seq(buf, send, recv):
        def step(i, carry):
            copy_start(buf.at[s], buf.at[s], send, recv, (d, seq_peer(i)))
            return carry

        lax.fori_loop(1, nseq, step, 0)

    def total_of(buf, n):
        parts = [buf[i].astype(F32) for i in range(n)]
        while len(parts) > 1:
            parts = [a + b for a, b in zip(parts[::2], parts[1::2])]
        return parts[0]

    wait_bytes(rret, dp_recv.at[4])
    mixed = t_mm(pack[...], rret[...]).astype(BF)
    for f in range(2):
        full = t_mm(
            mixed[f * tok : (f + 1) * tok, :], up_ref[:, f * half_width : (f + 1) * half_width]
        )
        for g in range(2):
            total = jnp.zeros((RANK, HEAD), F32)
            for h in range(g * RATIO, (g + 1) * RATIO):
                total = total + full[h * RANK : (h + 1) * RANK, h * HEAD : (h + 1) * HEAD]
            u_s[2 * f + g] = (2.0 * total).astype(BF)
    apart = ndp // KV
    owner = d % apart == 0
    for t in range(KV):

        @pl.when(d != t * apart)
        def _():
            copy_start(u_s.at[t], u_r.at[d], u_send.at[t], u_recv.at[0], (t * apart, s))

        @pl.when(d == t * apart)
        def _():
            pltpu.make_async_copy(u_s.at[t], u_r.at[d], u_recv.at[0]).start()

    n_share = g_s.shape[2]
    wait_bytes(rrg, dp_recv.at[5])
    rg_rows = t_mm(small[...], from_lines(rrg[...]).astype(BF)).astype(BF)
    rg_rows = mm(rg_rows, fold).astype(BF)
    grad = t_mm(rg_rows[:, :RANK], hidden_ref[...])
    for t in range(ndp):
        g_s[t] = grad[:, t * n_share : (t + 1) * n_share].astype(BF)

    def spread(src_of, dst, phase):
        def step(i, carry):
            p = dp_peer(i)
            copy_start(src_of(p), dst.at[d], ar_send.at[phase], ar_recv.at[phase], (p, s))
            return carry

        lax.fori_loop(1, ndp, step, 0)

    spread(lambda p: g_s.at[p], g_r, 0)
    pltpu.make_async_copy(g_s.at[d], g_r.at[d], ar_recv.at[0]).start()

    @pl.when(owner)
    def _():
        wait_bytes(u_r, u_recv.at[0])
        u_t[s] = total_of(u_r, ndp).astype(BF)
        to_seq(u_t, u_send.at[KV], u_recv.at[1])

    wait_bytes(g_r, ar_recv.at[0])
    g_t[s] = total_of(g_r, ndp).astype(BF)
    to_seq(g_t, ar_send.at[1], ar_recv.at[1])

    mine_t = d // apart

    @pl.when(owner)
    def _():
        wait_bytes(u_t.at[pl.ds(0, nseq - 1)], u_recv.at[1])
        u_a[mine_t] = total_of(u_t, nseq).astype(BF)

        def step(i, carry):
            copy_start(
                u_a.at[mine_t],
                u_a.at[mine_t],
                u_send.at[KV + 1],
                u_recv.at[2],
                (dp_peer(i), s),
            )
            return carry

        lax.fori_loop(1, ndp, step, 0)

    wait_bytes(g_t.at[pl.ds(0, nseq - 1)], ar_recv.at[1])
    g_a[d] = total_of(g_t, nseq).astype(BF)
    spread(lambda p: g_a.at[d], g_a, 2)

    @pl.when(owner)
    def _():
        wait_bytes(u_a.at[pl.ds(0, KV - 1)], u_recv.at[2])

    @pl.when(jnp.logical_not(owner))
    def _():
        wait_bytes(u_a, u_recv.at[2])

    for t in range(KV):
        upg_ref[:, t * HEAD : (t + 1) * HEAD] = u_a[t].astype(F32)
    wait_bytes(g_a.at[pl.ds(0, ndp - 1)], ar_recv.at[2])
    for t in range(ndp):
        gdown_ref[:, t * n_share : (t + 1) * n_share] = g_a[t].astype(F32)

    for kind, buf in enumerate((sa0, sb0, sa1, sb1, sret)):
        wait_sent(buf, dp_send.at[kind])
    wait_sent(sb2, dp_send.at[7])
    att_copy.wait()
    wait_sent(srg, dp_send.at[5], per_peer)
    wait_sent(sx, dp_send.at[6], per_peer)
    for piece, buf in enumerate((wa, wb)):
        for hop in range(1, hops + 1):
            ring(piece, buf, hop).wait_send()
        for hop in range(hops + 1):
            sibling(piece, buf, hop).wait_send()
    for w in range(back):
        rg_copy(w).wait_send()
    wait_bytes(g_s.at[pl.ds(0, ndp - 1)], ar_send.at[0])
    wait_bytes(g_t.at[pl.ds(0, nseq - 1)], ar_send.at[1])
    wait_bytes(g_a.at[pl.ds(0, ndp - 1)], ar_send.at[2])
    for t in range(KV):

        @pl.when(d != t * apart)
        def _():
            wait_bytes(u_s.at[t], u_send.at[t])

    @pl.when(owner)
    def _():
        wait_bytes(u_t.at[pl.ds(0, nseq - 1)], u_send.at[KV])
        wait_bytes(u_r.at[pl.ds(0, ndp - 1)], u_send.at[KV + 1])


def hand_over(a, b, c, a_out, b_out, c_out):
    a_out[...] = a[...]
    b_out[...] = b[...]
    c_out[...] = c[...]


def shards(nx, hops, hidden, q, k, v, up, group, slot, labels, down, upw):
    ndp = lax.axis_size("dp")
    nseq = lax.axis_size("seq")
    tok = hidden.shape[0]
    slots = 4 * tok
    back = 2 * hops
    lines = 2 * tok // SPAN
    share = hidden.shape[1] // ndp
    dma = pltpu.SemaphoreType.DMA
    widths = (2 * HEAD, 2 * HEAD, 5 * HEAD, 2 * HEAD, 2 * HEAD)
    scratch = (
        [pltpu.VMEM((slots, n), BF) for n in widths]
        + [pltpu.VMEM((slots, n), BF) for n in widths]
        + [
            pltpu.VMEM(((back + 2) * tok, 5 * HEAD), BF),
            pltpu.VMEM(((back + 2) * tok, 4 * HEAD), BF),
            pltpu.VMEM((2, RATIO * tok, (back + 1) * tok), BF),
            pltpu.VMEM((tok, (back + 1) * tok), F32),
            pltpu.VMEM((2 * tok, HEAD), BF),
        ]
        + [pltpu.VMEM((slots, HEAD), BF)] * 2
        + [pltpu.VMEM((lines, 2, HEAD), F32)] * 2
        + [pltpu.VMEM((lines, 1, HEAD), F32)] * 2
        + [pltpu.VMEM((back * RANK, tok), BF)] * 2
        + [
            pltpu.VMEM((ndp, RANK, share), BF),
            pltpu.VMEM((ndp, RANK, share), BF),
            pltpu.VMEM((nseq, RANK, share), BF),
            pltpu.VMEM((ndp, RANK, share), BF),
            pltpu.VMEM((KV, RANK, HEAD), BF),
            pltpu.VMEM((ndp, RANK, HEAD), BF),
            pltpu.VMEM((nseq, RANK, HEAD), BF),
            pltpu.VMEM((KV, RANK, HEAD), BF),
            dma((8,)),
            dma((8,)),
            dma((2, hops + 1)),
            dma((2, hops + 1)),
            dma((2, hops + 1)),
            dma((2, hops + 1)),
            dma((back,)),
            dma((back,)),
            dma((3,)),
            dma((3,)),
            dma((KV + 2,)),
            dma((3,)),
            pltpu.VMEM((2 * tok, tok), BF),
            pltpu.VMEM((2 * tok, tok), BF),
            pltpu.VMEM((slots, 2 * tok), BF),
            pltpu.VMEM((slots, 2 * tok), BF),
            pltpu.VMEM((2 * tok, slots), BF),
            pltpu.VMEM((tok, KV * HEAD), BF),
        ]
        + [pltpu.VMEM(a.shape, BF) for a in (hidden, q, k, v, up, q)]
        + [dma((6,))]
    )
    vmem = pl.BlockSpec(memory_space=pltpu.VMEM)
    anywhere = pl.BlockSpec(memory_space=pl.ANY)
    results = pl.pallas_call(
        functools.partial(kernel, ndp, nx, nseq, hops),
        out_shape=(
            jax.ShapeDtypeStruct(q.shape, BF),
            jax.ShapeDtypeStruct(down.shape, F32),
            jax.ShapeDtypeStruct(upw.shape, F32),
        ),
        in_specs=[anywhere] * 5 + [vmem] * 5,
        out_specs=(anywhere, vmem, vmem),
        scratch_shapes=scratch,
        compiler_params=pltpu.CompilerParams(
            collective_id=0, has_side_effects=True, vmem_limit_bytes=56 * 1024 * 1024
        ),
        cost_estimate=pl.CostEstimate(
            flops=4 * 10**9, bytes_accessed=4 * 10**6, transcendentals=2400000
        ),
    )(
        hidden,
        q,
        k,
        v,
        up,
        group.reshape(1, tok),
        slot.reshape(1, tok),
        labels,
        down,
        upw,
    )
    return pl.pallas_call(
        hand_over,
        out_shape=tuple(jax.ShapeDtypeStruct(a.shape, a.dtype) for a in results),
        in_specs=[vmem] * 3,
        out_specs=(vmem,) * 3,
        cost_estimate=pl.CostEstimate(flops=0, bytes_accessed=1600000, transcendentals=0),
    )(*results)


def build(mesh, nx, hops):
    rows = P(("dp", "seq"), None)
    return jax.shard_map(
        functools.partial(shards, nx, hops),
        mesh=mesh,
        in_specs=(
            rows,
            rows,
            rows,
            rows,
            rows,
            P(("dp", "seq")),
            P(("dp", "seq")),
            P("dp", "seq"),
            P(),
            P(),
        ),
        out_specs=(rows, P(), P()),
        check_vma=False,
    )


def solution(mesh):
    return build(mesh, 4, 4)
```

```python
import functools
import math

import jax
import jax.numpy as jnp
from jax import lax
from jax.experimental import pallas as pl
from jax.experimental.pallas import tpu as pltpu
from jax.sharding import PartitionSpec as P

MESH = pl.DeviceIdType.MESH
BF = jnp.bfloat16
F32 = jnp.float32
HEAD = 128
RANK = 16
KV = 4
RATIO = 4
ONE_LANE = 16
SPAN = HEAD // RANK


def mm(a, b):
    return jnp.dot(a, b, preferred_element_type=F32)


def mm_t(a, b):
    return lax.dot_general(a, b, (((1,), (1,)), ((), ())), preferred_element_type=F32)


def t_mm(a, b):
    return lax.dot_general(a, b, (((0,), (0,)), ((), ())), preferred_element_type=F32)


def iota(shape, dim):
    return lax.broadcasted_iota(jnp.int32, shape, dim)


def kernel(
    ndp,
    nx,
    nseq,
    hops,
    hidden_in,
    q_in,
    k_in,
    v_in,
    up_in,
    group_ref,
    slot_ref,
    label_ref,
    down_ref,
    upw_ref,
    att_out,
    gdown_ref,
    upg_ref,
    sk0,
    sv0,
    sk1,
    sv1,
    sa1,
    sb1,
    sb2,
    rk0,
    rv0,
    rk1,
    rv1,
    ra1,
    rb1,
    rb2,
    wk0,
    wv0,
    wk1,
    wv1,
    wx,
    pbuf,
    bias,
    aret,
    sret,
    rret,
    sx,
    rx,
    srg,
    rrg,
    rgs,
    rgr,
    g_s,
    g_r,
    g_t,
    g_a,
    u_s,
    u_r,
    u_t,
    u_a,
    dp_send,
    dp_recv,
    ring_send,
    ring_recv,
    sib_send,
    sib_recv,
    rg_send,
    rg_recv,
    ar_send,
    ar_recv,
    u_send,
    u_recv,
    small,
    unsmall,
    pack,
    unpack,
    unpack_t,
    value_ref,
    hidden_ref,
    q_ref,
    k_ref,
    v_ref,
    up_ref,
    att_ref,
    load,
):
    tok = hidden_ref.shape[0]
    loads = [
        pltpu.make_async_copy(src, dst, load.at[i])
        for i, (src, dst) in enumerate(
            (
                (hidden_in, hidden_ref),
                (k_in, k_ref),
                (v_in, v_ref),
                (q_in, q_ref),
                (up_in, up_ref),
            )
        )
    ]
    att_copy = pltpu.make_async_copy(att_ref, att_out, load.at[5])
    for copy in loads:
        copy.start()
    nz = ndp // nx
    ny = nseq // 2
    cap = 2 * tok // ndp
    blk = 2 * cap
    slots = ndp * blk
    back = 2 * hops
    win = (back + 1) * tok
    d = lax.axis_index("dp")
    s = lax.axis_index("seq")
    z, x = d // nx, d % nx
    y, c = s // 2, s % 2

    def far_first(i, n):
        return (n + n // 2 + ((i + 1) // 2) * (2 * ((i + 1) % 2) - 1)) % n

    def dp_peer(step):
        i = step - 1
        return ((z + far_first(i // nx, nz)) % nz) * nx + (x + far_first(i % nx, nx)) % nx

    def seq_peer(step):
        i = step - 1
        return ((y + far_first(i // 2, ny)) % ny) * 2 + (c + 1 - i % 2) % 2

    barrier = pltpu.get_barrier_semaphore()

    def greet_dp(step, carry):
        pl.semaphore_signal(barrier, inc=1, device_id=(dp_peer(step), s), device_id_type=MESH)
        return carry

    def greet_seq(step, carry):
        pl.semaphore_signal(barrier, inc=1, device_id=(d, seq_peer(step)), device_id_type=MESH)
        return carry

    lax.fori_loop(1, ndp, greet_dp, 0)
    lax.fori_loop(1, nseq, greet_seq, 0)

    def rows_of(index, size):
        return pl.ds(pl.multiple_of(index * size, size), size)

    def send_dp(src, dst, kind, size=blk):
        def step(i, carry):
            p = dp_peer(i)
            pltpu.make_async_remote_copy(
                src_ref=src.at[rows_of(p, size)],
                dst_ref=dst.at[rows_of(d, size)],
                send_sem=dp_send.at[kind],
                recv_sem=dp_recv.at[kind],
                device_id=(p, s),
                device_id_type=MESH,
            ).start()
            return carry

        lax.fori_loop(1, ndp, step, 0)
        here = rows_of(d, size)
        pltpu.make_async_copy(src.at[here], dst.at[here], dp_recv.at[kind]).start()

    def wait_bytes(ref, sem):
        pltpu.make_async_copy(ref, ref, sem).wait()

    def wait_sent(ref, sem, size=blk):
        wait_bytes(ref.at[pl.ds(0, (ndp - 1) * size)], sem)

    lane = iota((tok, tok), 1)
    sub = iota((tok, tok), 0)
    grow = jnp.broadcast_to(group_ref[...].astype(F32), (tok, tok))
    same = (grow == grow.T) & (sub < lane)
    rank = jnp.sum(jnp.where(same, 1.0, 0.0), axis=0, keepdims=True)
    place = group_ref[...].astype(F32) * cap + rank
    srow = iota((slots, tok), 0)
    half_row = (srow % blk) // cap
    slot_id = ((srow // blk) * cap + srow % cap).astype(F32)
    hit = slot_id == place
    for f in range(2):
        pack[:, f * tok : (f + 1) * tok] = jnp.where(hit & (half_row == f), 1.0, 0.0).astype(BF)

    n_small = slots // 2
    lines = n_small // SPAN
    per_peer = lines // ndp
    mine = iota((n_small, HEAD), 1) // RANK == iota((n_small, HEAD), 0) % SPAN

    def to_lines(rows):
        kept = jnp.where(mine, rows, 0.0).reshape(lines, SPAN, HEAD)
        return jnp.sum(kept, axis=1, keepdims=True)

    def from_lines(line):
        spread = jnp.broadcast_to(line, (lines, SPAN, HEAD)).reshape(n_small, HEAD)
        return jnp.where(mine, spread, 0.0)

    fold = (sub % RANK == lane) & (lane < RANK)
    fold = jnp.where(fold, 1.0, 0.0).astype(BF)
    small_id = iota((n_small, tok), 0).astype(F32)
    small[...] = jnp.where(small_id == place, 1.0, 0.0).astype(BF)

    down = jnp.concatenate([down_ref[...]] * SPAN, axis=0)
    loads[0].wait()
    reduced = mm_t(hidden_ref[...], down).astype(BF)
    upw = upw_ref[...]
    upw_full = jnp.concatenate([upw, jnp.zeros((HEAD - RANK, upw.shape[1]), BF)], axis=0)
    loads[2].wait()
    value = (v_ref[...].astype(F32) + 2.0 * mm(reduced, upw_full)).astype(BF)
    value_ref[...] = value
    slot_col = jnp.broadcast_to(slot_ref[...].astype(F32), (tok, tok)).T
    sx[:, 0:1, :] = to_lines(mm(small[...], reduced))
    sx[:, 1:2, :] = to_lines(mm(small[...], (slot_col + 1.0).astype(BF)))

    def kv_cols(rows, cc):
        return rows[:, cc * HEAD : (cc + 1) * HEAD]

    loads[1].wait()

    def both_halves(ref, first):
        return jnp.concatenate([kv_cols(ref[...], 2 * f + first) for f in range(2)], axis=0)

    sk0[...] = mm(pack[...], both_halves(k_ref, 0)).astype(BF)
    pl.semaphore_wait(barrier, ndp + nseq - 2)
    send_dp(sk0, rk0, 0)
    send_dp(sx, rx, 6, per_peer)
    sv0[...] = mm(pack[...], both_halves(value_ref, 0)).astype(BF)
    send_dp(sv0, rv0, 1)
    sk1[...] = mm(pack[...], both_halves(k_ref, 1)).astype(BF)
    send_dp(sk1, rk1, 8)
    sv1[...] = mm(pack[...], both_halves(value_ref, 1)).astype(BF)
    send_dp(sv1, rv1, 9)

    half_heads = KV * RATIO // 2
    half_width = half_heads * HEAD
    diag = iota((HEAD, half_width), 0) // RANK == iota((HEAD, half_width), 1) // HEAD
    narrow = []
    loads[4].wait()
    for f in range(2):
        wide = jnp.concatenate(
            [kv_cols(upw, 2 * f + h // RATIO) for h in range(half_heads)], axis=1
        ).astype(F32)
        wide = jnp.concatenate([wide] * half_heads, axis=0)
        wide = jnp.where(diag, wide, 0.0).astype(BF)
        narrow.append(mm_t(up_ref[:, f * half_width : (f + 1) * half_width], wide).astype(BF))
    quad = RATIO * HEAD

    def q_cols(cc):
        return q_ref[:, cc * quad : (cc + 1) * quad]

    loads[3].wait()
    xa1 = jnp.concatenate(
        [jnp.concatenate([q_cols(2 * f), narrow[f]], axis=1) for f in range(2)], axis=0
    )
    sa1[...] = mm(pack[...], xa1).astype(BF)
    send_dp(sa1, ra1, 2)
    xb1 = jnp.concatenate([q_cols(2 * f + 1) for f in range(2)], axis=0)
    sb1[...] = mm(pack[...], xb1[:, : quad // 2]).astype(BF)
    send_dp(sb1, rb1, 3)
    sb2[...] = mm(pack[...], xb1[:, quad // 2 :]).astype(BF)
    send_dp(sb2, rb2, 7)

    def place_of(hop, core, buf):
        return rows_of((hops - hop) * 2 + core, buf.shape[0] // (back + 2))

    def ring(piece, buf, hop):
        return pltpu.make_async_remote_copy(
            src_ref=buf.at[place_of(hop - 1, c, buf)],
            dst_ref=buf.at[place_of(hop, c, buf)],
            send_sem=ring_send.at[piece, hop],
            recv_sem=ring_recv.at[piece, hop],
            device_id=(d, ((y + 1) % ny) * 2 + c),
            device_id_type=MESH,
        )

    def sibling(piece, buf, hop):
        return pltpu.make_async_remote_copy(
            src_ref=buf.at[place_of(hop, c, buf)],
            dst_ref=buf.at[place_of(hop, c, buf)],
            send_sem=sib_send.at[piece, hop],
            recv_sem=sib_recv.at[piece, hop],
            device_id=(d, y * 2 + 1 - c),
            device_id_type=MESH,
        )

    def sibling_arrived(piece, buf, hop):
        wait_bytes(buf.at[place_of(hop, 1 - c, buf)], sib_recv.at[piece, hop])

    wait_bytes(rx, dp_recv.at[6])
    slot_in = jnp.max(from_lines(rx[:, 1:2, :]), axis=1, keepdims=True)
    slot_in = jnp.broadcast_to(slot_in, (n_small, tok))
    at_small = jnp.where(slot_in == (iota((n_small, tok), 1) + 1).astype(F32), 1.0, 0.0)
    unsmall[...] = at_small.astype(BF)
    at = jnp.broadcast_to(at_small.reshape(ndp, 1, cap, tok), (ndp, 2, cap, tok))
    at = at.reshape(slots, tok)
    for f in range(2):
        chosen = jnp.where(half_row == f, at, 0.0)
        unpack[:, f * tok : (f + 1) * tok] = chosen.astype(BF)
        unpack_t[f * tok : (f + 1) * tok, :] = chosen.T.astype(BF)
    reduced_in = t_mm(unsmall[...], from_lines(rx[:, 0:1, :]).astype(BF)).astype(BF)
    fold_all = jnp.where(sub % RANK == lane % RANK, 1.0, 0.0).astype(BF)
    reduced_in = jnp.where(lane // RANK == sub % SPAN, mm(reduced_in, fold_all), 0.0)
    thin = tok // SPAN
    reduced_in = jnp.sum(reduced_in.reshape(thin, SPAN, HEAD), axis=1)
    doc_row = jnp.broadcast_to(label_ref[...].astype(F32), (thin, tok))
    wx[place_of(0, c, wx), :] = jnp.concatenate([reduced_in, doc_row], axis=0).astype(BF)
    pieces = ((0, wk0), (1, wx), (2, wv0), (3, wk1), (4, wv1))

    def set_out(piece, buf):
        ring(piece, buf, 1).start()
        sibling(piece, buf, 0).start()

    for piece, buf, arrived, kind in (
        (0, wk0, rk0, 0),
        (2, wv0, rv0, 1),
        (3, wk1, rk1, 8),
        (4, wv1, rv1, 9),
    ):
        wait_bytes(arrived, dp_recv.at[kind])
        arranged = mm(unpack_t[...], arrived[...]).astype(BF)
        buf[place_of(0, c, buf), :] = jnp.concatenate(
            [arranged[:tok, :], arranged[tok:, :]], axis=1
        )
        set_out(piece, buf)
        if piece == 0:
            set_out(1, wx)

    def pass_on(piece, buf, hop):
        ring(piece, buf, hop).wait_recv()
        if hop < hops:
            ring(piece, buf, hop + 1).start()
        sibling(piece, buf, hop).start()

    for hop in range(1, hops):
        for piece, buf in pieces:
            pass_on(piece, buf, hop)
    wait_bytes(ra1, dp_recv.at[2])
    queries = mm(unpack_t[...], ra1[...]).astype(BF)
    for piece, buf in pieces[:3]:
        pass_on(piece, buf, hops)
    for hop in range(hops + 1):
        for piece, buf in pieces[:3]:
            sibling_arrived(piece, buf, hop)

    window = pl.ds(pl.multiple_of(c * tok, tok), win)
    thin_win = pl.ds(pl.multiple_of(c * 2 * thin, 2 * thin), (back + 1) * 2 * thin)
    thin_rows = wx[thin_win, :].astype(F32).reshape(back + 1, 2 * thin, HEAD)
    doc_keys = jnp.concatenate([thin_rows[w, thin : thin + 1] for w in range(back + 1)], axis=1)
    doc_col = jnp.broadcast_to(label_ref[...].astype(F32), (tok, tok)).T
    together = doc_col[:, 0:1] == doc_keys
    n_thin = (back + 1) * thin
    tiles = thin_rows[:, :thin].reshape(n_thin, 1, HEAD)
    tiles = jnp.broadcast_to(tiles, (n_thin, SPAN, HEAD)).reshape(win, HEAD)
    win_lane = iota((win, HEAD), 1)
    tiles = jnp.where(win_lane // RANK == iota((win, HEAD), 0) % SPAN, tiles, 0.0).astype(BF)
    tiles = jnp.where(win_lane == ONE_LANE, 1.0, mm(tiles, fold)).astype(BF)
    col = iota((tok, win), 1)
    seen = together & (col - back * tok <= iota((tok, win), 0)) & (col >= (back - s) * tok)
    bias[...] = jnp.where(seen, 0.0, -1e30)
    scale = math.log2(math.e) / math.sqrt(HEAD)

    narrow_in = [queries[f * tok : (f + 1) * tok, quad:].astype(F32) for f in range(2)]
    returned = [jnp.zeros((tok, HEAD), F32) for _ in range(2)]

    def attend(piece, wk, wv, arranged, f, first, count):
        cc = 2 * f + piece
        key = wk[window, f * HEAD : (f + 1) * HEAD]
        val = jnp.concatenate([wv[window, f * HEAD : (f + 1) * HEAD], tiles], axis=1)
        query = jnp.concatenate(
            [
                arranged[f * tok : (f + 1) * tok, h * HEAD : (h + 1) * HEAD]
                for h in range(count)
            ],
            axis=0,
        )
        scores = mm_t(query, key)
        for h in range(count):
            part = scores[h * tok : (h + 1) * tok, :] * scale + bias[...]
            top = jnp.max(part, axis=1, keepdims=True)
            pbuf[f, h * tok : (h + 1) * tok, :] = jnp.exp2(part - top).astype(BF)
        weights = pbuf[f, : count * tok, :]
        out = mm(weights, val)
        inv = 1.0 / out[:, HEAD + ONE_LANE : HEAD + ONE_LANE + 1]
        attended = (out[:, :HEAD] * inv).astype(BF)
        mixed = jnp.where(iota((count * tok, HEAD), 1) < RANK, out[:, HEAD:] * inv, 0.0)
        lefts = []
        for h in range(count):
            head = cc * RATIO + first + h
            lanes = (piece * RATIO + first + h) * RANK
            rows = slice(h * tok, (h + 1) * tok)
            att_ref[:, head * HEAD : (head + 1) * HEAD] = attended[rows]
            moved = pltpu.roll(mixed[rows], lanes, 1) if lanes else mixed[rows]
            returned[f] = returned[f] + moved
            left = narrow_in[f]
            left = pltpu.roll(left, HEAD - lanes, 1) if lanes else left
            lefts.append((left[:, :RANK] * inv[rows]).astype(BF))
        return t_mm(jnp.concatenate(lefts, axis=0), weights)

    half = RATIO // 2
    rg_total = attend(0, wk0, wv0, queries, 0, 0, RATIO)
    for piece, buf in pieces[3:]:
        pass_on(piece, buf, hops)
    rg_total = rg_total + attend(0, wk0, wv0, queries, 1, 0, RATIO)
    for hop in range(hops + 1):
        for piece, buf in pieces[3:]:
            sibling_arrived(piece, buf, hop)
    for arrived, kind, first in ((rb1, 3, 0), (rb2, 7, half)):
        wait_bytes(arrived, dp_recv.at[kind])
        queries = mm(unpack_t[...], arrived[...]).astype(BF)
        for f in range(2):
            rg_total = rg_total + attend(1, wk1, wv1, queries, f, first, half)
    att_copy.start()

    def rg_copy(w):
        return pltpu.make_async_remote_copy(
            src_ref=rgs.at[w * RANK : (w + 1) * RANK],
            dst_ref=rgr.at[w * RANK : (w + 1) * RANK],
            send_sem=rg_send.at[w],
            recv_sem=rg_recv.at[w],
            device_id=(d, (s + nseq - back + w) % nseq),
            device_id_type=MESH,
        )

    for w in range(back):
        rgs[w * RANK : (w + 1) * RANK, :] = rg_total[:, w * tok : (w + 1) * tok].astype(BF)
    for w in range(back):
        rg_copy(w).start()
    rg_own = rg_total[:, back * tok :]

    aret[:tok, :] = returned[0].astype(BF)
    aret[tok:, :] = returned[1].astype(BF)
    sret[...] = mm(unpack[...], aret[...]).astype(BF)
    send_dp(sret, rret, 4)

    for w in range(back):
        rg_copy(w).wait_recv()
        rg_own = rg_own + rgr[w * RANK : (w + 1) * RANK, :].astype(F32)
    rg_own = jnp.concatenate([(2.0 * rg_own).astype(BF)] * SPAN, axis=0)
    srg[...] = to_lines(mm_t(unsmall[...], rg_own))
    send_dp(srg, rrg, 5, per_peer)

    def copy_start(src, dst, send, recv, target):
        pltpu.make_async_remote_copy(
            src_ref=src,
            dst_ref=dst,
            send_sem=send,
            recv_sem=recv,
            device_id=target,
            device_id_type=MESH,
        ).start()

    def to_seq(buf, send, recv):
        def step(i, carry):
            copy_start(buf.at[s], buf.at[s], send, recv, (d, seq_peer(i)))
            return carry

        lax.fori_loop(1, nseq, step, 0)

    def total_of(buf, n):
        parts = [buf[i].astype(F32) for i in range(n)]
        while len(parts) > 1:
            parts = [a + b for a, b in zip(parts[::2], parts[1::2])]
        return parts[0]

    wait_bytes(rret, dp_recv.at[4])
    mixed = t_mm(pack[...], rret[...]).astype(BF)
    for f in range(2):
        full = t_mm(
            mixed[f * tok : (f + 1) * tok, :], up_ref[:, f * half_width : (f + 1) * half_width]
        )
        for g in range(2):
            total = jnp.zeros((RANK, HEAD), F32)
            for h in range(g * RATIO, (g + 1) * RATIO):
                total = total + full[h * RANK : (h + 1) * RANK, h * HEAD : (h + 1) * HEAD]
            u_s[2 * f + g] = (2.0 * total).astype(BF)
    apart = ndp // KV
    owner = d % apart == 0
    for t in range(KV):

        @pl.when(d != t * apart)
        def _():
            copy_start(u_s.at[t], u_r.at[d], u_send.at[t], u_recv.at[0], (t * apart, s))

        @pl.when(d == t * apart)
        def _():
            pltpu.make_async_copy(u_s.at[t], u_r.at[d], u_recv.at[0]).start()

    n_share = g_s.shape[2]
    wait_bytes(rrg, dp_recv.at[5])
    rg_rows = t_mm(small[...], from_lines(rrg[...]).astype(BF)).astype(BF)
    rg_rows = mm(rg_rows, fold).astype(BF)
    grad = t_mm(rg_rows[:, :RANK], hidden_ref[...])
    for t in range(ndp):
        g_s[t] = grad[:, t * n_share : (t + 1) * n_share].astype(BF)

    def spread(src_of, dst, phase):
        def step(i, carry):
            p = dp_peer(i)
            copy_start(src_of(p), dst.at[d], ar_send.at[phase], ar_recv.at[phase], (p, s))
            return carry

        lax.fori_loop(1, ndp, step, 0)

    spread(lambda p: g_s.at[p], g_r, 0)
    pltpu.make_async_copy(g_s.at[d], g_r.at[d], ar_recv.at[0]).start()

    @pl.when(owner)
    def _():
        wait_bytes(u_r, u_recv.at[0])
        u_t[s] = total_of(u_r, ndp).astype(BF)
        to_seq(u_t, u_send.at[KV], u_recv.at[1])

    wait_bytes(g_r, ar_recv.at[0])
    g_t[s] = total_of(g_r, ndp).astype(BF)
    to_seq(g_t, ar_send.at[1], ar_recv.at[1])

    mine_t = d // apart

    @pl.when(owner)
    def _():
        wait_bytes(u_t.at[pl.ds(0, nseq - 1)], u_recv.at[1])
        u_a[mine_t] = total_of(u_t, nseq).astype(BF)

        def step(i, carry):
            copy_start(
                u_a.at[mine_t],
                u_a.at[mine_t],
                u_send.at[KV + 1],
                u_recv.at[2],
                (dp_peer(i), s),
            )
            return carry

        lax.fori_loop(1, ndp, step, 0)

    wait_bytes(g_t.at[pl.ds(0, nseq - 1)], ar_recv.at[1])
    g_a[d] = total_of(g_t, nseq).astype(BF)
    spread(lambda p: g_a.at[d], g_a, 2)

    @pl.when(owner)
    def _():
        wait_bytes(u_a.at[pl.ds(0, KV - 1)], u_recv.at[2])

    @pl.when(jnp.logical_not(owner))
    def _():
        wait_bytes(u_a, u_recv.at[2])

    for t in range(KV):
        upg_ref[:, t * HEAD : (t + 1) * HEAD] = u_a[t].astype(F32)
    wait_bytes(g_a.at[pl.ds(0, ndp - 1)], ar_recv.at[2])
    for t in range(ndp):
        gdown_ref[:, t * n_share : (t + 1) * n_share] = g_a[t].astype(F32)

    for kind, buf in (
        (0, sk0),
        (1, sv0),
        (8, sk1),
        (9, sv1),
        (2, sa1),
        (3, sb1),
        (7, sb2),
        (4, sret),
    ):
        wait_sent(buf, dp_send.at[kind])
    att_copy.wait()
    wait_sent(srg, dp_send.at[5], per_peer)
    wait_sent(sx, dp_send.at[6], per_peer)
    for piece, buf in pieces:
        for hop in range(1, hops + 1):
            ring(piece, buf, hop).wait_send()
        for hop in range(hops + 1):
            sibling(piece, buf, hop).wait_send()
    for w in range(back):
        rg_copy(w).wait_send()
    wait_bytes(g_s.at[pl.ds(0, ndp - 1)], ar_send.at[0])
    wait_bytes(g_t.at[pl.ds(0, nseq - 1)], ar_send.at[1])
    wait_bytes(g_a.at[pl.ds(0, ndp - 1)], ar_send.at[2])
    for t in range(KV):

        @pl.when(d != t * apart)
        def _():
            wait_bytes(u_s.at[t], u_send.at[t])

    @pl.when(owner)
    def _():
        wait_bytes(u_t.at[pl.ds(0, nseq - 1)], u_send.at[KV])
        wait_bytes(u_r.at[pl.ds(0, ndp - 1)], u_send.at[KV + 1])


def hand_over(a, b, c, a_out, b_out, c_out):
    a_out[...] = a[...]
    b_out[...] = b[...]
    c_out[...] = c[...]


def shards(nx, hops, hidden, q, k, v, up, group, slot, labels, down, upw):
    ndp = lax.axis_size("dp")
    nseq = lax.axis_size("seq")
    tok = hidden.shape[0]
    slots = 4 * tok
    back = 2 * hops
    lines = 2 * tok // SPAN
    share = hidden.shape[1] // ndp
    dma = pltpu.SemaphoreType.DMA
    widths = (HEAD, HEAD, HEAD, HEAD, 5 * HEAD, 2 * HEAD, 2 * HEAD)
    scratch = (
        [pltpu.VMEM((slots, n), BF) for n in widths]
        + [pltpu.VMEM((slots, n), BF) for n in widths]
        + [
            pltpu.VMEM(((back + 2) * tok, 2 * HEAD), BF),
            pltpu.VMEM(((back + 2) * tok, 2 * HEAD), BF),
            pltpu.VMEM(((back + 2) * tok, 2 * HEAD), BF),
            pltpu.VMEM(((back + 2) * tok, 2 * HEAD), BF),
            pltpu.VMEM(((back + 2) * 2 * (tok // SPAN), HEAD), BF),
            pltpu.VMEM((2, RATIO * tok, (back + 1) * tok), BF),
            pltpu.VMEM((tok, (back + 1) * tok), F32),
            pltpu.VMEM((2 * tok, HEAD), BF),
        ]
        + [pltpu.VMEM((slots, HEAD), BF)] * 2
        + [pltpu.VMEM((lines, 2, HEAD), F32)] * 2
        + [pltpu.VMEM((lines, 1, HEAD), F32)] * 2
        + [pltpu.VMEM((back * RANK, tok), BF)] * 2
        + [
            pltpu.VMEM((ndp, RANK, share), BF),
            pltpu.VMEM((ndp, RANK, share), BF),
            pltpu.VMEM((nseq, RANK, share), BF),
            pltpu.VMEM((ndp, RANK, share), BF),
            pltpu.VMEM((KV, RANK, HEAD), BF),
            pltpu.VMEM((ndp, RANK, HEAD), BF),
            pltpu.VMEM((nseq, RANK, HEAD), BF),
            pltpu.VMEM((KV, RANK, HEAD), BF),
            dma((10,)),
            dma((10,)),
            dma((5, hops + 1)),
            dma((5, hops + 1)),
            dma((5, hops + 1)),
            dma((5, hops + 1)),
            dma((back,)),
            dma((back,)),
            dma((3,)),
            dma((3,)),
            dma((KV + 2,)),
            dma((3,)),
            pltpu.VMEM((2 * tok, tok), BF),
            pltpu.VMEM((2 * tok, tok), BF),
            pltpu.VMEM((slots, 2 * tok), BF),
            pltpu.VMEM((slots, 2 * tok), BF),
            pltpu.VMEM((2 * tok, slots), BF),
            pltpu.VMEM((tok, KV * HEAD), BF),
        ]
        + [pltpu.VMEM(a.shape, BF) for a in (hidden, q, k, v, up, q)]
        + [dma((6,))]
    )
    vmem = pl.BlockSpec(memory_space=pltpu.VMEM)
    anywhere = pl.BlockSpec(memory_space=pl.ANY)
    results = pl.pallas_call(
        functools.partial(kernel, ndp, nx, nseq, hops),
        out_shape=(
            jax.ShapeDtypeStruct(q.shape, BF),
            jax.ShapeDtypeStruct(down.shape, F32),
            jax.ShapeDtypeStruct(upw.shape, F32),
        ),
        in_specs=[anywhere] * 5 + [vmem] * 5,
        out_specs=(anywhere, vmem, vmem),
        scratch_shapes=scratch,
        compiler_params=pltpu.CompilerParams(
            collective_id=0, has_side_effects=True, vmem_limit_bytes=56 * 1024 * 1024
        ),
        cost_estimate=pl.CostEstimate(
            flops=4 * 10**9, bytes_accessed=4 * 10**6, transcendentals=2400000
        ),
    )(
        hidden,
        q,
        k,
        v,
        up,
        group.reshape(1, tok),
        slot.reshape(1, tok),
        labels,
        down,
        upw,
    )
    return pl.pallas_call(
        hand_over,
        out_shape=tuple(jax.ShapeDtypeStruct(a.shape, a.dtype) for a in results),
        in_specs=[vmem] * 3,
        out_specs=(vmem,) * 3,
        cost_estimate=pl.CostEstimate(flops=0, bytes_accessed=1600000, transcendentals=0),
    )(*results)


def build(mesh, nx, hops):
    rows = P(("dp", "seq"), None)
    return jax.shard_map(
        functools.partial(shards, nx, hops),
        mesh=mesh,
        in_specs=(
            rows,
            rows,
            rows,
            rows,
            rows,
            P(("dp", "seq")),
            P(("dp", "seq")),
            P("dp", "seq"),
            P(),
            P(),
        ),
        out_specs=(rows, P(), P()),
        check_vma=False,
    )


def solution(mesh):
    return build(mesh, 4, 4)
```

```python
import functools
import math

import jax
import jax.numpy as jnp
from jax import lax
from jax.experimental import pallas as pl
from jax.experimental.pallas import tpu as pltpu
from jax.sharding import PartitionSpec as P

MESH = pl.DeviceIdType.MESH
BF = jnp.bfloat16
F32 = jnp.float32
HEAD = 128
RANK = 16
KV = 4
RATIO = 4
ONE_LANE = 16
SPAN = HEAD // RANK


def mm(a, b):
    return jnp.dot(a, b, preferred_element_type=F32)


def mm_t(a, b):
    return lax.dot_general(a, b, (((1,), (1,)), ((), ())), preferred_element_type=F32)


def t_mm(a, b):
    return lax.dot_general(a, b, (((0,), (0,)), ((), ())), preferred_element_type=F32)


def iota(shape, dim):
    return lax.broadcasted_iota(jnp.int32, shape, dim)


def kernel(
    ndp,
    nx,
    nseq,
    hops,
    hidden_in,
    q_in,
    k_in,
    v_in,
    up_in,
    group_ref,
    slot_ref,
    label_ref,
    down_ref,
    upw_ref,
    att_out,
    gdown_ref,
    upg_ref,
    sk0,
    sv0,
    sk1,
    sv1,
    sa1,
    sb1,
    rk0,
    rv0,
    rk1,
    rv1,
    ra1,
    rb1,
    wk0,
    wv0,
    wk1,
    wv1,
    wx,
    pbuf,
    bias,
    aret,
    sret,
    rret,
    sx,
    rx,
    srg,
    rrg,
    rgs,
    rgr,
    g_s,
    g_r,
    g_t,
    g_a,
    u_s,
    u_r,
    u_t,
    u_a,
    dp_send,
    dp_recv,
    ring_send,
    ring_recv,
    sib_send,
    sib_recv,
    rg_send,
    rg_recv,
    ar_send,
    ar_recv,
    u_send,
    u_recv,
    small,
    unsmall,
    pack,
    unpack,
    unpack_t,
    value_ref,
    hidden_ref,
    q_ref,
    k_ref,
    v_ref,
    up_ref,
    att_ref,
    load,
):
    tok = hidden_ref.shape[0]
    loads = [
        pltpu.make_async_copy(src, dst, load.at[i])
        for i, (src, dst) in enumerate(
            (
                (hidden_in, hidden_ref),
                (k_in, k_ref),
                (v_in, v_ref),
                (q_in, q_ref),
                (up_in, up_ref),
            )
        )
    ]
    att_copy = pltpu.make_async_copy(att_ref, att_out, load.at[5])
    for copy in loads:
        copy.start()
    nz = ndp // nx
    ny = nseq // 2
    cap = 2 * tok // ndp
    blk = 2 * cap
    slots = ndp * blk
    back = 2 * hops
    win = (back + 1) * tok
    d = lax.axis_index("dp")
    s = lax.axis_index("seq")
    z, x = d // nx, d % nx
    y, c = s // 2, s % 2

    def far_first(i, n):
        return (n + n // 2 + ((i + 1) // 2) * (2 * ((i + 1) % 2) - 1)) % n

    def dp_peer(step):
        i = step - 1
        return ((z + far_first(i // nx, nz)) % nz) * nx + (x + far_first(i % nx, nx)) % nx

    def seq_peer(step):
        i = step - 1
        return ((y + far_first(i // 2, ny)) % ny) * 2 + (c + 1 - i % 2) % 2

    barrier = pltpu.get_barrier_semaphore()

    def greet_dp(step, carry):
        pl.semaphore_signal(barrier, inc=1, device_id=(dp_peer(step), s), device_id_type=MESH)
        return carry

    def greet_seq(step, carry):
        pl.semaphore_signal(barrier, inc=1, device_id=(d, seq_peer(step)), device_id_type=MESH)
        return carry

    lax.fori_loop(1, ndp, greet_dp, 0)
    lax.fori_loop(1, nseq, greet_seq, 0)

    def rows_of(index, size):
        return pl.ds(pl.multiple_of(index * size, size), size)

    def send_dp(src, dst, kind, size=blk):
        def step(i, carry):
            p = dp_peer(i)
            pltpu.make_async_remote_copy(
                src_ref=src.at[rows_of(p, size)],
                dst_ref=dst.at[rows_of(d, size)],
                send_sem=dp_send.at[kind],
                recv_sem=dp_recv.at[kind],
                device_id=(p, s),
                device_id_type=MESH,
            ).start()
            return carry

        lax.fori_loop(1, ndp, step, 0)
        here = rows_of(d, size)
        pltpu.make_async_copy(src.at[here], dst.at[here], dp_recv.at[kind]).start()

    def wait_bytes(ref, sem):
        pltpu.make_async_copy(ref, ref, sem).wait()

    def wait_sent(ref, sem, size=blk):
        wait_bytes(ref.at[pl.ds(0, (ndp - 1) * size)], sem)

    lane = iota((tok, tok), 1)
    sub = iota((tok, tok), 0)
    grow = jnp.broadcast_to(group_ref[...].astype(F32), (tok, tok))
    same = (grow == grow.T) & (sub < lane)
    rank = jnp.sum(jnp.where(same, 1.0, 0.0), axis=0, keepdims=True)
    place = group_ref[...].astype(F32) * cap + rank
    srow = iota((slots, tok), 0)
    half_row = (srow % blk) // cap
    slot_id = ((srow // blk) * cap + srow % cap).astype(F32)
    hit = slot_id == place
    for f in range(2):
        pack[:, f * tok : (f + 1) * tok] = jnp.where(hit & (half_row == f), 1.0, 0.0).astype(BF)

    n_small = slots // 2
    lines = n_small // SPAN
    per_peer = lines // ndp
    mine = iota((n_small, HEAD), 1) // RANK == iota((n_small, HEAD), 0) % SPAN

    def to_lines(rows):
        kept = jnp.where(mine, rows, 0.0).reshape(lines, SPAN, HEAD)
        return jnp.sum(kept, axis=1, keepdims=True)

    def from_lines(line):
        spread = jnp.broadcast_to(line, (lines, SPAN, HEAD)).reshape(n_small, HEAD)
        return jnp.where(mine, spread, 0.0)

    fold = (sub % RANK == lane) & (lane < RANK)
    fold = jnp.where(fold, 1.0, 0.0).astype(BF)
    small_id = iota((n_small, tok), 0).astype(F32)
    small[...] = jnp.where(small_id == place, 1.0, 0.0).astype(BF)

    down = jnp.concatenate([down_ref[...]] * SPAN, axis=0)
    loads[0].wait()
    reduced = mm_t(hidden_ref[...], down).astype(BF)
    upw = upw_ref[...]
    upw_full = jnp.concatenate([upw, jnp.zeros((HEAD - RANK, upw.shape[1]), BF)], axis=0)
    loads[2].wait()
    value = (v_ref[...].astype(F32) + 2.0 * mm(reduced, upw_full)).astype(BF)
    value_ref[...] = value
    slot_col = jnp.broadcast_to(slot_ref[...].astype(F32), (tok, tok)).T
    sx[:, 0:1, :] = to_lines(mm(small[...], reduced))
    sx[:, 1:2, :] = to_lines(mm(small[...], (slot_col + 1.0).astype(BF)))

    def kv_cols(rows, cc):
        return rows[:, cc * HEAD : (cc + 1) * HEAD]

    loads[1].wait()

    def both_halves(ref, first):
        return jnp.concatenate([kv_cols(ref[...], 2 * f + first) for f in range(2)], axis=0)

    sk0[...] = mm(pack[...], both_halves(k_ref, 0)).astype(BF)
    pl.semaphore_wait(barrier, ndp + nseq - 2)
    send_dp(sk0, rk0, 0)
    send_dp(sx, rx, 6, per_peer)
    sv0[...] = mm(pack[...], both_halves(value_ref, 0)).astype(BF)
    send_dp(sv0, rv0, 1)
    sk1[...] = mm(pack[...], both_halves(k_ref, 1)).astype(BF)
    send_dp(sk1, rk1, 8)
    sv1[...] = mm(pack[...], both_halves(value_ref, 1)).astype(BF)
    send_dp(sv1, rv1, 9)

    half_heads = KV * RATIO // 2
    half_width = half_heads * HEAD
    diag = iota((HEAD, half_width), 0) // RANK == iota((HEAD, half_width), 1) // HEAD
    narrow = []
    loads[4].wait()
    for f in range(2):
        wide = jnp.concatenate(
            [kv_cols(upw, 2 * f + h // RATIO) for h in range(half_heads)], axis=1
        ).astype(F32)
        wide = jnp.concatenate([wide] * half_heads, axis=0)
        wide = jnp.where(diag, wide, 0.0).astype(BF)
        narrow.append(mm_t(up_ref[:, f * half_width : (f + 1) * half_width], wide).astype(BF))
    quad = RATIO * HEAD

    def q_cols(cc):
        return q_ref[:, cc * quad : (cc + 1) * quad]

    loads[3].wait()
    xa1 = jnp.concatenate(
        [jnp.concatenate([q_cols(2 * f), narrow[f]], axis=1) for f in range(2)], axis=0
    )
    sa1[...] = mm(pack[...], xa1).astype(BF)
    send_dp(sa1, ra1, 2)
    xb1 = jnp.concatenate([q_cols(2 * f + 1) for f in range(2)], axis=0)
    sb1[...] = mm(pack[...], xb1).astype(BF)
    send_dp(sb1, rb1, 3)

    def place_of(hop, core, buf):
        return rows_of((hops - hop) * 2 + core, buf.shape[0] // (back + 2))

    def ring(piece, buf, hop):
        return pltpu.make_async_remote_copy(
            src_ref=buf.at[place_of(hop - 1, c, buf)],
            dst_ref=buf.at[place_of(hop, c, buf)],
            send_sem=ring_send.at[piece, hop],
            recv_sem=ring_recv.at[piece, hop],
            device_id=(d, ((y + 1) % ny) * 2 + c),
            device_id_type=MESH,
        )

    def sibling(piece, buf, hop):
        return pltpu.make_async_remote_copy(
            src_ref=buf.at[place_of(hop, c, buf)],
            dst_ref=buf.at[place_of(hop, c, buf)],
            send_sem=sib_send.at[piece, hop],
            recv_sem=sib_recv.at[piece, hop],
            device_id=(d, y * 2 + 1 - c),
            device_id_type=MESH,
        )

    def sibling_arrived(piece, buf, hop):
        wait_bytes(buf.at[place_of(hop, 1 - c, buf)], sib_recv.at[piece, hop])

    wait_bytes(rx, dp_recv.at[6])
    slot_in = jnp.max(from_lines(rx[:, 1:2, :]), axis=1, keepdims=True)
    slot_in = jnp.broadcast_to(slot_in, (n_small, tok))
    at_small = jnp.where(slot_in == (iota((n_small, tok), 1) + 1).astype(F32), 1.0, 0.0)
    unsmall[...] = at_small.astype(BF)
    at = jnp.broadcast_to(at_small.reshape(ndp, 1, cap, tok), (ndp, 2, cap, tok))
    at = at.reshape(slots, tok)
    for f in range(2):
        chosen = jnp.where(half_row == f, at, 0.0)
        unpack[:, f * tok : (f + 1) * tok] = chosen.astype(BF)
        unpack_t[f * tok : (f + 1) * tok, :] = chosen.T.astype(BF)
    reduced_in = t_mm(unsmall[...], from_lines(rx[:, 0:1, :]).astype(BF)).astype(BF)
    fold_all = jnp.where(sub % RANK == lane % RANK, 1.0, 0.0).astype(BF)
    reduced_in = jnp.where(lane // RANK == sub % SPAN, mm(reduced_in, fold_all), 0.0)
    thin = tok // SPAN
    reduced_in = jnp.sum(reduced_in.reshape(thin, SPAN, HEAD), axis=1)
    doc_row = jnp.broadcast_to(label_ref[...].astype(F32), (thin, tok))
    wx[place_of(0, c, wx), :] = jnp.concatenate([reduced_in, doc_row], axis=0).astype(BF)
    pieces = ((0, wk0), (1, wx), (2, wv0), (3, wk1), (4, wv1))

    def set_out(piece, buf):
        ring(piece, buf, 1).start()
        sibling(piece, buf, 0).start()

    for piece, buf, arrived, kind in (
        (0, wk0, rk0, 0),
        (2, wv0, rv0, 1),
        (3, wk1, rk1, 8),
        (4, wv1, rv1, 9),
    ):
        wait_bytes(arrived, dp_recv.at[kind])
        arranged = mm(unpack_t[...], arrived[...]).astype(BF)
        buf[place_of(0, c, buf), :] = jnp.concatenate(
            [arranged[:tok, :], arranged[tok:, :]], axis=1
        )
        set_out(piece, buf)
        if piece == 0:
            set_out(1, wx)

    def pass_on(piece, buf, hop):
        ring(piece, buf, hop).wait_recv()
        if hop < hops:
            ring(piece, buf, hop + 1).start()
        sibling(piece, buf, hop).start()

    for hop in range(1, hops):
        for piece, buf in pieces:
            pass_on(piece, buf, hop)
    wait_bytes(ra1, dp_recv.at[2])
    queries = mm(unpack_t[...], ra1[...]).astype(BF)
    for piece, buf in pieces[:3]:
        pass_on(piece, buf, hops)
    for hop in range(hops + 1):
        for piece, buf in pieces[:3]:
            sibling_arrived(piece, buf, hop)

    window = pl.ds(pl.multiple_of(c * tok, tok), win)
    thin_win = pl.ds(pl.multiple_of(c * 2 * thin, 2 * thin), (back + 1) * 2 * thin)
    thin_rows = wx[thin_win, :].astype(F32).reshape(back + 1, 2 * thin, HEAD)
    doc_keys = jnp.concatenate([thin_rows[w, thin : thin + 1] for w in range(back + 1)], axis=1)
    doc_col = jnp.broadcast_to(label_ref[...].astype(F32), (tok, tok)).T
    together = doc_col[:, 0:1] == doc_keys
    n_thin = (back + 1) * thin
    tiles = thin_rows[:, :thin].reshape(n_thin, 1, HEAD)
    tiles = jnp.broadcast_to(tiles, (n_thin, SPAN, HEAD)).reshape(win, HEAD)
    win_lane = iota((win, HEAD), 1)
    tiles = jnp.where(win_lane // RANK == iota((win, HEAD), 0) % SPAN, tiles, 0.0).astype(BF)
    tiles = jnp.where(win_lane == ONE_LANE, 1.0, mm(tiles, fold)).astype(BF)
    col = iota((tok, win), 1)
    seen = together & (col - back * tok <= iota((tok, win), 0)) & (col >= (back - s) * tok)
    bias[...] = jnp.where(seen, 0.0, -1e30)
    scale = math.log2(math.e) / math.sqrt(HEAD)

    narrow_in = [queries[f * tok : (f + 1) * tok, quad:].astype(F32) for f in range(2)]
    returned = [jnp.zeros((tok, HEAD), F32) for _ in range(2)]

    def attend(piece, wk, wv, arranged, f, first, count):
        cc = 2 * f + piece
        key = wk[window, f * HEAD : (f + 1) * HEAD]
        val = jnp.concatenate([wv[window, f * HEAD : (f + 1) * HEAD], tiles], axis=1)
        query = jnp.concatenate(
            [
                arranged[f * tok : (f + 1) * tok, h * HEAD : (h + 1) * HEAD]
                for h in range(count)
            ],
            axis=0,
        )
        scores = mm_t(query, key)
        for h in range(count):
            part = scores[h * tok : (h + 1) * tok, :] * scale + bias[...]
            top = jnp.max(part, axis=1, keepdims=True)
            pbuf[f, h * tok : (h + 1) * tok, :] = jnp.exp2(part - top).astype(BF)
        weights = pbuf[f, : count * tok, :]
        out = mm(weights, val)
        inv = 1.0 / out[:, HEAD + ONE_LANE : HEAD + ONE_LANE + 1]
        attended = (out[:, :HEAD] * inv).astype(BF)
        mixed = jnp.where(iota((count * tok, HEAD), 1) < RANK, out[:, HEAD:] * inv, 0.0)
        lefts = []
        for h in range(count):
            head = cc * RATIO + first + h
            lanes = (piece * RATIO + first + h) * RANK
            rows = slice(h * tok, (h + 1) * tok)
            att_ref[:, head * HEAD : (head + 1) * HEAD] = attended[rows]
            moved = pltpu.roll(mixed[rows], lanes, 1) if lanes else mixed[rows]
            returned[f] = returned[f] + moved
            left = narrow_in[f]
            left = pltpu.roll(left, HEAD - lanes, 1) if lanes else left
            lefts.append((left[:, :RANK] * inv[rows]).astype(BF))
        return t_mm(jnp.concatenate(lefts, axis=0), weights)

    rg_total = attend(0, wk0, wv0, queries, 0, 0, RATIO)
    for piece, buf in pieces[3:]:
        pass_on(piece, buf, hops)
    rg_total = rg_total + attend(0, wk0, wv0, queries, 1, 0, RATIO)
    for hop in range(hops + 1):
        for piece, buf in pieces[3:]:
            sibling_arrived(piece, buf, hop)
    wait_bytes(rb1, dp_recv.at[3])
    queries = mm(unpack_t[...], rb1[...]).astype(BF)
    for f in range(2):
        rg_total = rg_total + attend(1, wk1, wv1, queries, f, 0, RATIO)
    att_copy.start()

    def rg_copy(w):
        return pltpu.make_async_remote_copy(
            src_ref=rgs.at[w * RANK : (w + 1) * RANK],
            dst_ref=rgr.at[w * RANK : (w + 1) * RANK],
            send_sem=rg_send.at[w],
            recv_sem=rg_recv.at[w],
            device_id=(d, (s + nseq - back + w) % nseq),
            device_id_type=MESH,
        )

    for w in range(back):
        rgs[w * RANK : (w + 1) * RANK, :] = rg_total[:, w * tok : (w + 1) * tok].astype(BF)
    for w in range(back):
        rg_copy(w).start()
    rg_own = rg_total[:, back * tok :]

    aret[:tok, :] = returned[0].astype(BF)
    aret[tok:, :] = returned[1].astype(BF)
    sret[...] = mm(unpack[...], aret[...]).astype(BF)
    send_dp(sret, rret, 4)

    for w in range(back):
        rg_copy(w).wait_recv()
        rg_own = rg_own + rgr[w * RANK : (w + 1) * RANK, :].astype(F32)
    rg_own = jnp.concatenate([(2.0 * rg_own).astype(BF)] * SPAN, axis=0)
    srg[...] = to_lines(mm_t(unsmall[...], rg_own))
    send_dp(srg, rrg, 5, per_peer)

    def copy_start(src, dst, send, recv, target):
        pltpu.make_async_remote_copy(
            src_ref=src,
            dst_ref=dst,
            send_sem=send,
            recv_sem=recv,
            device_id=target,
            device_id_type=MESH,
        ).start()

    def to_seq(buf, send, recv):
        def step(i, carry):
            copy_start(buf.at[s], buf.at[s], send, recv, (d, seq_peer(i)))
            return carry

        lax.fori_loop(1, nseq, step, 0)

    def total_of(buf, n):
        parts = [buf[i].astype(F32) for i in range(n)]
        while len(parts) > 1:
            parts = [a + b for a, b in zip(parts[::2], parts[1::2])]
        return parts[0]

    wait_bytes(rret, dp_recv.at[4])
    mixed = t_mm(pack[...], rret[...]).astype(BF)
    for f in range(2):
        full = t_mm(
            mixed[f * tok : (f + 1) * tok, :], up_ref[:, f * half_width : (f + 1) * half_width]
        )
        for g in range(2):
            total = jnp.zeros((RANK, HEAD), F32)
            for h in range(g * RATIO, (g + 1) * RATIO):
                total = total + full[h * RANK : (h + 1) * RANK, h * HEAD : (h + 1) * HEAD]
            u_s[2 * f + g] = (2.0 * total).astype(BF)
    apart = ndp // KV
    owner = d % apart == 0
    for t in range(KV):

        @pl.when(d != t * apart)
        def _():
            copy_start(u_s.at[t], u_r.at[d], u_send.at[t], u_recv.at[0], (t * apart, s))

        @pl.when(d == t * apart)
        def _():
            pltpu.make_async_copy(u_s.at[t], u_r.at[d], u_recv.at[0]).start()

    n_share = g_s.shape[2]
    wait_bytes(rrg, dp_recv.at[5])
    rg_rows = t_mm(small[...], from_lines(rrg[...]).astype(BF)).astype(BF)
    rg_rows = mm(rg_rows, fold).astype(BF)
    grad = t_mm(rg_rows[:, :RANK], hidden_ref[...])
    for t in range(ndp):
        g_s[t] = grad[:, t * n_share : (t + 1) * n_share].astype(BF)

    def spread(src_of, dst, phase):
        def step(i, carry):
            p = dp_peer(i)
            copy_start(src_of(p), dst.at[d], ar_send.at[phase], ar_recv.at[phase], (p, s))
            return carry

        lax.fori_loop(1, ndp, step, 0)

    spread(lambda p: g_s.at[p], g_r, 0)
    pltpu.make_async_copy(g_s.at[d], g_r.at[d], ar_recv.at[0]).start()

    @pl.when(owner)
    def _():
        wait_bytes(u_r, u_recv.at[0])
        u_t[s] = total_of(u_r, ndp).astype(BF)
        to_seq(u_t, u_send.at[KV], u_recv.at[1])

    wait_bytes(g_r, ar_recv.at[0])
    g_t[s] = total_of(g_r, ndp).astype(BF)
    to_seq(g_t, ar_send.at[1], ar_recv.at[1])

    mine_t = d // apart

    @pl.when(owner)
    def _():
        wait_bytes(u_t.at[pl.ds(0, nseq - 1)], u_recv.at[1])
        u_a[mine_t] = total_of(u_t, nseq).astype(BF)

        def step(i, carry):
            copy_start(
                u_a.at[mine_t],
                u_a.at[mine_t],
                u_send.at[KV + 1],
                u_recv.at[2],
                (dp_peer(i), s),
            )
            return carry

        lax.fori_loop(1, ndp, step, 0)

    wait_bytes(g_t.at[pl.ds(0, nseq - 1)], ar_recv.at[1])
    g_a[d] = total_of(g_t, nseq).astype(BF)
    spread(lambda p: g_a.at[d], g_a, 2)

    @pl.when(owner)
    def _():
        wait_bytes(u_a.at[pl.ds(0, KV - 1)], u_recv.at[2])

    @pl.when(jnp.logical_not(owner))
    def _():
        wait_bytes(u_a, u_recv.at[2])

    upg_ref[...] = u_a[...]
    wait_bytes(g_a.at[pl.ds(0, ndp - 1)], ar_recv.at[2])
    gdown_ref[...] = g_a[...]

    for kind, buf in (
        (0, sk0),
        (1, sv0),
        (8, sk1),
        (9, sv1),
        (2, sa1),
        (3, sb1),
        (4, sret),
    ):
        wait_sent(buf, dp_send.at[kind])
    att_copy.wait()
    wait_sent(srg, dp_send.at[5], per_peer)
    wait_sent(sx, dp_send.at[6], per_peer)
    for piece, buf in pieces:
        for hop in range(1, hops + 1):
            ring(piece, buf, hop).wait_send()
        for hop in range(hops + 1):
            sibling(piece, buf, hop).wait_send()
    for w in range(back):
        rg_copy(w).wait_send()
    wait_bytes(g_s.at[pl.ds(0, ndp - 1)], ar_send.at[0])
    wait_bytes(g_t.at[pl.ds(0, nseq - 1)], ar_send.at[1])
    wait_bytes(g_a.at[pl.ds(0, ndp - 1)], ar_send.at[2])
    for t in range(KV):

        @pl.when(d != t * apart)
        def _():
            wait_bytes(u_s.at[t], u_send.at[t])

    @pl.when(owner)
    def _():
        wait_bytes(u_t.at[pl.ds(0, nseq - 1)], u_send.at[KV])
        wait_bytes(u_r.at[pl.ds(0, ndp - 1)], u_send.at[KV + 1])


def hand_over(att, down, up, att_out, down_out, up_out):
    att_out[...] = att[...]
    for part, out in ((down, down_out), (up, up_out)):
        width = part.shape[2]
        for t in range(part.shape[0]):
            out[:, t * width : (t + 1) * width] = part[t].astype(F32)


def shards(nx, hops, hidden, q, k, v, up, group, slot, labels, down, upw):
    ndp = lax.axis_size("dp")
    nseq = lax.axis_size("seq")
    tok = hidden.shape[0]
    slots = 4 * tok
    back = 2 * hops
    lines = 2 * tok // SPAN
    share = hidden.shape[1] // ndp
    dma = pltpu.SemaphoreType.DMA
    widths = (HEAD, HEAD, HEAD, HEAD, 5 * HEAD, 4 * HEAD)
    scratch = (
        [pltpu.VMEM((slots, n), BF) for n in widths]
        + [pltpu.VMEM((slots, n), BF) for n in widths]
        + [
            pltpu.VMEM(((back + 2) * tok, 2 * HEAD), BF),
            pltpu.VMEM(((back + 2) * tok, 2 * HEAD), BF),
            pltpu.VMEM(((back + 2) * tok, 2 * HEAD), BF),
            pltpu.VMEM(((back + 2) * tok, 2 * HEAD), BF),
            pltpu.VMEM(((back + 2) * 2 * (tok // SPAN), HEAD), BF),
            pltpu.VMEM((2, RATIO * tok, (back + 1) * tok), BF),
            pltpu.VMEM((tok, (back + 1) * tok), F32),
            pltpu.VMEM((2 * tok, HEAD), BF),
        ]
        + [pltpu.VMEM((slots, HEAD), BF)] * 2
        + [pltpu.VMEM((lines, 2, HEAD), F32)] * 2
        + [pltpu.VMEM((lines, 1, HEAD), F32)] * 2
        + [pltpu.VMEM((back * RANK, tok), BF)] * 2
        + [
            pltpu.VMEM((ndp, RANK, share), BF),
            pltpu.VMEM((ndp, RANK, share), BF),
            pltpu.VMEM((nseq, RANK, share), BF),
            pltpu.VMEM((ndp, RANK, share), BF),
            pltpu.VMEM((KV, RANK, HEAD), BF),
            pltpu.VMEM((ndp, RANK, HEAD), BF),
            pltpu.VMEM((nseq, RANK, HEAD), BF),
            pltpu.VMEM((KV, RANK, HEAD), BF),
            dma((10,)),
            dma((10,)),
            dma((5, hops + 1)),
            dma((5, hops + 1)),
            dma((5, hops + 1)),
            dma((5, hops + 1)),
            dma((back,)),
            dma((back,)),
            dma((3,)),
            dma((3,)),
            dma((KV + 2,)),
            dma((3,)),
            pltpu.VMEM((2 * tok, tok), BF),
            pltpu.VMEM((2 * tok, tok), BF),
            pltpu.VMEM((slots, 2 * tok), BF),
            pltpu.VMEM((slots, 2 * tok), BF),
            pltpu.VMEM((2 * tok, slots), BF),
            pltpu.VMEM((tok, KV * HEAD), BF),
        ]
        + [pltpu.VMEM(a.shape, BF) for a in (hidden, q, k, v, up, q)]
        + [dma((6,))]
    )
    vmem = pl.BlockSpec(memory_space=pltpu.VMEM)
    anywhere = pl.BlockSpec(memory_space=pl.ANY)
    results = pl.pallas_call(
        functools.partial(kernel, ndp, nx, nseq, hops),
        out_shape=(
            jax.ShapeDtypeStruct(q.shape, BF),
            jax.ShapeDtypeStruct((ndp, RANK, share), BF),
            jax.ShapeDtypeStruct((KV, RANK, HEAD), BF),
        ),
        in_specs=[anywhere] * 5 + [vmem] * 5,
        out_specs=(anywhere, vmem, vmem),
        scratch_shapes=scratch,
        compiler_params=pltpu.CompilerParams(
            collective_id=0, has_side_effects=True, vmem_limit_bytes=56 * 1024 * 1024
        ),
        cost_estimate=pl.CostEstimate(
            flops=4 * 10**9, bytes_accessed=4 * 10**6, transcendentals=2400000
        ),
    )(
        hidden,
        q,
        k,
        v,
        up,
        group.reshape(1, tok),
        slot.reshape(1, tok),
        labels,
        down,
        upw,
    )
    return pl.pallas_call(
        hand_over,
        out_shape=(
            jax.ShapeDtypeStruct(q.shape, BF),
            jax.ShapeDtypeStruct(down.shape, F32),
            jax.ShapeDtypeStruct(upw.shape, F32),
        ),
        in_specs=[vmem] * 3,
        out_specs=(vmem,) * 3,
        cost_estimate=pl.CostEstimate(flops=0, bytes_accessed=1600000, transcendentals=0),
    )(*results)


def build(mesh, nx, hops):
    rows = P(("dp", "seq"), None)
    return jax.shard_map(
        functools.partial(shards, nx, hops),
        mesh=mesh,
        in_specs=(
            rows,
            rows,
            rows,
            rows,
            rows,
            P(("dp", "seq")),
            P(("dp", "seq")),
            P("dp", "seq"),
            P(),
            P(),
        ),
        out_specs=(rows, P(), P()),
        check_vma=False,
    )


def solution(mesh):
    return build(mesh, 4, 4)
```
